512 devices in a mesh: seq: 32 (over y_lo, x, core), fsdp: 16 (over y_hi, z).
Axes of the slice: x: 4, y: 8 (y_hi: 2, y_lo: 4; y = y_hi * 4 + y_lo), z: 8, core: 2. Of those that a mesh axis runs over, the one named last changes fastest.
Arguments:
- query_raw: bfloat16 [16, 4096, 4096], P('fsdp', 'seq'), may hold values from -8 to 8
- key_raw: bfloat16 [16, 4096, 1024], P('fsdp', 'seq'), may hold values from -8 to 8
- value_proj: bfloat16 [16, 4096, 1024], P('fsdp', 'seq'), may hold values from -6 to 6
- out_grad: bfloat16 [16, 4096, 4096], P('fsdp', 'seq'), may hold values from -6 to 6
- query_gain: float32 [128], P('fsdp'), may hold values from 0.5 to 3.8
- key_gain: float32 [128], P('fsdp'), may hold values from 0.5 to 3.8
- turn_lengths: int32 [16, 48], P('fsdp'), may hold values from 1 to 256, 4096 in all within a row
Outputs:
- query_raw_grad: bfloat16 [16, 4096, 4096], P('fsdp', 'seq')
- key_raw_grad: bfloat16 [16, 4096, 1024], P('fsdp', 'seq')
- value_grad: bfloat16 [16, 4096, 1024], P('fsdp', 'seq')
- query_gain_grad: float32 [128], P('fsdp')
- key_gain_grad: float32 [128], P('fsdp')
The draws below stay inside these ranges and needn't reach their ends.
Inputs may be any that keep to these rules, and one draw needn't show every extreme that they name: `turn_lengths`: each row sums to 4096; no turn is longer than 256 tokens, and every trajectory has a turn of exactly 256.
All inputs are finite; a program needn't handle non-finite values.
Results may differ from the reference program's by a relative error of at most 0.0264.
The reference program's roundings to bfloat16 on the way (of `probs_low`, `dscore` and `dquery`) count: a program that leaves them out, or rounds other values in their place, can miss the bound.
Values may be sent and summed in bfloat16 or wider, within the bound.
No kernel may reach another device: no remote copies, remote signals or barrier semaphores. Data moves between devices by JAX's collectives and lax.ppermute only.
A program may use at most 128 MiB of HBM per device.

```python
import math
import jax
import jax.numpy as jnp
import numpy as np
from jax import lax

HEADS = 32
KV_HEADS = 8
HEAD_DIM = 128
TURNS = 48
SEQ_LEN = 4096
TURN = 256
TRAJ = 16


def draw_query_raw(key, part):
    key = jax.random.fold_in(key, 11)
    noise = jnp.clip(jax.random.normal(key, (TRAJ, SEQ_LEN, HEADS, HEAD_DIM), jnp.float32), -4.0, 4.0)
    return noise.reshape(TRAJ, SEQ_LEN, HEADS * HEAD_DIM).astype(jnp.bfloat16)


def draw_key_raw(key, part):
    key = jax.random.fold_in(key, 12)
    noise = jnp.clip(jax.random.normal(key, (TRAJ, SEQ_LEN, KV_HEADS, HEAD_DIM), jnp.float32), -4.0, 4.0)
    return noise.reshape(TRAJ, SEQ_LEN, KV_HEADS * HEAD_DIM).astype(jnp.bfloat16)


def draw_query_gain(key, part):
    key = jax.random.fold_in(key, 13)
    return jax.random.uniform(key, (HEAD_DIM,), jnp.float32, 0.5, 2.0)


def draw_key_gain(key, part):
    key = jax.random.fold_in(key, 14)
    return jax.random.uniform(key, (HEAD_DIM,), jnp.float32, 0.5, 2.0)


def steps_of(rng, dims, cuts, low, high):
    def one(axis_at, shards_of):
        heights = jax.random.uniform(jax.random.fold_in(jax.random.fold_in(rng, 6), axis_at), (shards_of,), jnp.float32, low / len(cuts), high / len(cuts))
        return jnp.repeat(jnp.exp(heights), dims[axis_at] // shards_of).reshape((-1,) + (1,) * (len(dims) - axis_at - 1))

    level = one(*cuts[0])
    for cut in cuts[1:]:
        level = level * one(*cut)
    return level


def length_profile(amount, total, limit, skew):
    loads = [(1 << 20) // math.isqrt(grade ** skew) + 1 for grade in range(2, amount + 1)]
    rest, counts = total - limit - (amount - 1), [1] * (amount - 1)
    while rest > 0:
        movable = [i for i in range(amount - 1) if counts[i] < limit]
        pool, left = sum([loads[i] for i in movable]), rest
        for i in movable:
            extra = min(limit - counts[i], max(1, left * loads[i] // pool), rest)
            counts[i] = counts[i] + extra
            rest = rest - extra
    return np.array([limit] + counts)


def uneven_parts(stream_key, count, total, most, slope):
    if count == 2:
        one = jax.random.randint(stream_key, (), max(1, total - most), min(most, total - 1) + 1)
        return jnp.stack([one, total - one])
    sizes = jnp.asarray(length_profile(count, total, most, slope), jnp.int32)
    twos = (count - 1) // 2
    donor, receiver = sizes[1:1 + 2 * twos:2], sizes[2:2 + 2 * twos:2]
    room = jnp.minimum(donor - 1, most - receiver)
    shifted = jax.random.randint(jax.random.fold_in(stream_key, 1), (twos,), 0, 1 << 20) % (room + 1)
    sizes = sizes.at[1:1 + 2 * twos:2].set(donor - shifted).at[2:2 + 2 * twos:2].set(receiver + shifted)
    return sizes[jax.random.permutation(jax.random.fold_in(stream_key, 2), count)]


def scatter_about(key, dims, width, reach, pieces=(), kind=jnp.bfloat16):
    array = width * jax.random.normal(key, dims, jnp.float32)
    if pieces:
        array = array * steps_of(key, dims, pieces, -0.22, 0.18)
    return jnp.clip(array, -reach, reach).astype(kind)


def setup_inputs(seed: int = 0) -> dict:
    seeds = jax.random.split(jax.random.key(seed), 8)
    return {
        "query_raw": draw_query_raw(jax.random.fold_in(seeds[7], 71), 0),
        "key_raw": draw_key_raw(jax.random.fold_in(seeds[7], 71), 0),
        "value_proj": scatter_about(seeds[2], (TRAJ, SEQ_LEN, KV_HEADS * HEAD_DIM), 1.0, 6.0, ((0, 16), (1, 32))),
        "out_grad": scatter_about(seeds[3], (TRAJ, SEQ_LEN, HEADS * HEAD_DIM), 1.0, 6.0, ((0, 16), (1, 32))),
        "query_gain": draw_query_gain(jax.random.fold_in(seeds[7], 71), 0),
        "key_gain": draw_key_gain(jax.random.fold_in(seeds[7], 71), 0),
        "turn_lengths": jax.vmap(lambda own: uneven_parts(own, TURNS, SEQ_LEN, TURN, 0))(jax.random.split(seeds[6], TRAJ)).reshape((TRAJ, TURNS)).astype(jnp.int32),
    }


norm_epsilon = 1e-06
rope_base = 1000000.0

def rotary_tables(positions, head_size):
    half_size = head_size // 2
    freqs = rope_base ** (-(jnp.arange(half_size, dtype=jnp.float32) * 2.0 / head_size))
    angles = positions.astype(jnp.float32)[:, None] * freqs[None, :]
    angles = jnp.concatenate([angles, angles], axis=1)
    return (jnp.cos(angles)[:, None, :], jnp.sin(angles)[:, None, :])

def rotate_half(values):
    half_size = values.shape[-1] // 2
    return jnp.concatenate([-values[..., half_size:], values[..., :half_size]], axis=-1)

def rotate_back(values):
    half_size = values.shape[-1] // 2
    return jnp.concatenate([values[..., half_size:], -values[..., :half_size]], axis=-1)

def norm_forward(raw, gain, cosine, sine):
    values = raw.astype(jnp.float32)
    inverse = lax.rsqrt(lax.optimization_barrier(jnp.mean(values * values, axis=-1, keepdims=True)) + norm_epsilon)
    normed = values * inverse * gain
    rotated = normed * cosine + rotate_half(normed) * sine
    return (rotated.astype(jnp.bfloat16), values, inverse)

def norm_backward(grad_rot, values, inverse, gain, cosine, sine):
    grad_rot = grad_rot.astype(jnp.float32)
    grad_normed = grad_rot * cosine + rotate_back(grad_rot * sine)
    gain_part = lax.optimization_barrier(jnp.sum(grad_normed * values * inverse, axis=(0, 1)))
    scaled = grad_normed * gain
    grad_raw = inverse * (scaled - values * inverse * inverse * lax.optimization_barrier(jnp.mean(scaled * values, axis=-1, keepdims=True)))
    return (grad_raw.astype(jnp.bfloat16), gain_part)

def turn_ids(lengths, seq_len):
    ends = jnp.cumsum(lengths).astype(jnp.int32)
    positions = jnp.arange(seq_len, dtype=jnp.int32)
    return lax.optimization_barrier(jnp.sum((positions[:, None] >= ends[None, :]).astype(jnp.int32), axis=1))

def shift_blocks(values, count, fill):
    front = jnp.full((count,) + values.shape[1:], fill, values.dtype)
    return jnp.concatenate([front, values[:-count]], axis=0)

def unshift_blocks(values, count):
    back = jnp.zeros((count,) + values.shape[1:], values.dtype)
    return jnp.concatenate([values[count:], back], axis=0)

def window_of(blocks, fill):
    return jnp.concatenate([shift_blocks(blocks, 2, fill), shift_blocks(blocks, 1, fill), blocks], axis=1)

def attend(query, keys, values, dout, segment, seq_len):
    count = 32
    block = seq_len // count
    scale = HEAD_DIM ** (-0.5)
    query_blocks = query.astype(jnp.float32).reshape((count, block) + query.shape[1:])
    dout_blocks = dout.astype(jnp.float32).reshape((count, block) + dout.shape[1:])
    key_window = window_of(keys.astype(jnp.float32).reshape((count, block) + keys.shape[1:]), 0.0)
    value_window = window_of(values.astype(jnp.float32).reshape((count, block) + values.shape[1:]), 0.0)
    positions = jnp.arange(seq_len, dtype=jnp.int32).reshape(count, block)
    position_window = jnp.concatenate([positions - 2 * block, positions - block, positions], axis=1)
    segment_blocks = segment.reshape(count, block)
    segment_window = window_of(segment_blocks, -1)
    allowed = (position_window[:, None, :] <= positions[:, :, None]) & (position_window[:, None, :] >= 0) & (segment_window[:, None, :] == segment_blocks[:, :, None])
    allowed = allowed[:, None, None]
    scores = jnp.einsum('nqkgd,nwkd->nkgqw', query_blocks, key_window) * scale
    masked = jnp.where(allowed, scores, -jnp.inf)
    row_max = lax.optimization_barrier(jnp.max(masked, axis=-1, keepdims=True))
    weights = jnp.where(allowed, jnp.exp(masked - row_max), 0.0)
    probs = weights / lax.optimization_barrier(jnp.sum(weights, axis=-1, keepdims=True))
    probs_low = probs.astype(jnp.bfloat16)
    dprobs = jnp.einsum('nqkgd,nwkd->nkgqw', dout_blocks, value_window)
    delta = lax.optimization_barrier(jnp.sum(probs * dprobs, axis=-1, keepdims=True))
    dscore = (probs * (dprobs - delta) * scale).astype(jnp.bfloat16).astype(jnp.float32)
    dquery = jnp.einsum('nkgqw,nwkd->nqkgd', dscore, key_window).astype(jnp.bfloat16)
    dkey_window = jnp.einsum('nkgqw,nqkgd->nwkd', dscore, query_blocks)
    dvalue_window = jnp.einsum('nkgqw,nqkgd->nwkd', probs_low.astype(jnp.float32), dout_blocks)

    def fold_back(window):
        total = window[:, 2 * block:] + unshift_blocks(window[:, block:2 * block], 1) + unshift_blocks(window[:, :block], 2)
        return total.reshape((seq_len,) + window.shape[2:])
    return (dquery.reshape(query.shape), fold_back(dkey_window), fold_back(dvalue_window))

def reference(query_raw, key_raw, value_proj, out_grad, query_gain, key_gain, turn_lengths):
    group_size = HEADS // KV_HEADS
    positions = jnp.arange(SEQ_LEN, dtype=jnp.int32)
    cosine, sine = rotary_tables(positions, HEAD_DIM)

    def one_trajectory(inputs):
        q_raw, k_raw, v_proj, o_grad, lengths = inputs
        query, q_values, q_inverse = norm_forward(q_raw.reshape(SEQ_LEN, HEADS, HEAD_DIM), query_gain, cosine, sine)
        keys, k_values, k_inverse = norm_forward(k_raw.reshape(SEQ_LEN, KV_HEADS, HEAD_DIM), key_gain, cosine, sine)
        segment = turn_ids(lengths, SEQ_LEN)
        dquery, dkeys, dvalues = attend(query.reshape(SEQ_LEN, KV_HEADS, group_size, HEAD_DIM), keys, v_proj.reshape(SEQ_LEN, KV_HEADS, HEAD_DIM), o_grad.reshape(SEQ_LEN, KV_HEADS, group_size, HEAD_DIM), segment, SEQ_LEN)
        dquery = dquery.reshape(SEQ_LEN, HEADS, HEAD_DIM)
        q_grad, q_gain_part = norm_backward(dquery, q_values, q_inverse, query_gain, cosine, sine)
        k_grad, k_gain_part = norm_backward(dkeys.astype(jnp.bfloat16), k_values, k_inverse, key_gain, cosine, sine)
        v_grad = dvalues.astype(jnp.bfloat16)
        return (q_grad.reshape(SEQ_LEN, HEADS * HEAD_DIM), k_grad.reshape(SEQ_LEN, KV_HEADS * HEAD_DIM), v_grad.reshape(SEQ_LEN, KV_HEADS * HEAD_DIM), q_gain_part, k_gain_part)
    q_grads, k_grads, v_grads, q_gain_parts, k_gain_parts = lax.map(one_trajectory, (query_raw, key_raw, value_proj, out_grad, turn_lengths))
    return (q_grads, k_grads, v_grads, lax.optimization_barrier(jnp.sum(q_gain_parts, axis=0)), lax.optimization_barrier(jnp.sum(k_gain_parts, axis=0)))
```

```python
import jax
import jax.numpy as jnp
from jax import lax
from jax.experimental import pallas as pl
from jax.experimental.pallas import tpu as pltpu
from jax.sharding import PartitionSpec as P

HEADS = 32
KV_HEADS = 8
GROUP = HEADS // KV_HEADS
HEAD_DIM = 128
HALF = HEAD_DIM // 2
ROWS = 128

norm_epsilon = 1e-06
rope_base = 1000000.0
MASKED = -1e30

NT = (((1,), (1,)), ((), ()))
NN = (((1,), (0,)), ((), ()))
TN = (((0,), (0,)), ((), ()))


def dot(a, b, dims):
    return lax.dot_general(a, b, dims, preferred_element_type=jnp.float32)


def roll_half(x):
    return pltpu.roll(x, HALF, axis=1)


def forward_norm(raw, gain, cosine, sine):
    x = raw.astype(jnp.float32)
    inverse = lax.rsqrt(jnp.mean(x * x, axis=-1, keepdims=True) + norm_epsilon)
    y = x * inverse * gain
    return x, inverse, (y * cosine + roll_half(y) * sine).astype(jnp.bfloat16)


def unrotate(grad, cosine, sine):
    return grad * cosine - roll_half(grad) * sine


def fold8(x):
    return jnp.sum(x.reshape(x.shape[0] // 8, 8, x.shape[1]), axis=0)


def stack_heads(x):
    return jnp.concatenate([x[:, h * HEAD_DIM:(h + 1) * HEAD_DIM] for h in range(GROUP)], axis=0)


def table_kernel(len_ref, place_ref, bias_ref, late_ref, take_ref):
    shape = (ROWS, ROWS)
    base = place_ref[0]
    row = lax.broadcasted_iota(jnp.int32, shape, 0)
    lane = lax.broadcasted_iota(jnp.int32, shape, 1)
    here = lax.broadcasted_iota(jnp.int32, (8, ROWS), 1)
    first = jnp.zeros((8, ROWS), jnp.int32) - base
    end = -base
    for k in range(len_ref.shape[0] - 1):
        end = end + len_ref[k]
        first = jnp.where(here >= end, end, first)
    first = jnp.concatenate([first] * (ROWS // 8), axis=0)
    bias_ref[0] = jnp.where(row >= first + ROWS, 0.0, MASKED)
    own = (row <= lane) & (row >= first)
    bias_ref[1] = jnp.where(own | (row >= first + 2 * ROWS), 0.0, MASKED)
    late_ref[...] = jnp.where(first < -ROWS, 1.0, 0.0).T
    head = jnp.broadcast_to(first[:, 0:1], shape)
    take_ref[...] = jnp.where(row >= head + 2 * ROWS, 1.0, 0.0)


def block_tables(lengths, place):
    tile = jax.ShapeDtypeStruct((ROWS, ROWS), jnp.float32)
    smem = pl.BlockSpec(memory_space=pltpu.SMEM)
    return pl.pallas_call(
        table_kernel,
        in_specs=[smem, smem],
        out_shape=[jax.ShapeDtypeStruct((2, ROWS, ROWS), jnp.float32), tile, tile],
        name="tables",
    )(lengths, place)


def attend_kernel(
    q_ref, do_ref, own_k, own_v, one_k, one_v, two_k, two_v,
    cos_ref, sin_ref, bias_ref, late_ref, take_ref, gain_ref,
    dq_ref, ret1_ref, ret2_ref, keep_ref, gains_ref, total_ref,
):
    scale = HEAD_DIM ** (-0.5)
    step = pl.program_id(0)
    gain = jnp.sum(gain_ref[...], axis=0)
    qg, kg = gain[0:1], gain[1:2]
    cos0, sin0 = cos_ref[0], sin_ref[0]
    cos4 = jnp.concatenate([cos0] * GROUP, axis=0)
    sin4 = jnp.concatenate([sin0] * GROUP, axis=0)
    late = late_ref[...] > 0.0
    take = take_ref[...] > 0.0
    late4 = jnp.concatenate([late] * GROUP, axis=0)
    cos2 = jnp.where(take, cos_ref[2], cos0)
    sin2 = jnp.where(take, sin_ref[2], sin0)

    x, inv_q, q = forward_norm(stack_heads(q_ref[...]), qg, cos4, sin4)
    do = stack_heads(do_ref[...])
    zero = jnp.zeros_like(q)
    q_wide = jnp.concatenate([jnp.where(late4, zero, q), jnp.where(late4, q, zero)], axis=1)
    do_wide = jnp.concatenate([jnp.where(late4, zero, do), jnp.where(late4, do, zero)], axis=1)

    v0, v1 = own_v[...], one_v[...]
    xk0, inv0, k0 = forward_norm(own_k[...], kg, cos0, sin0)
    xk1, inv1, k1 = forward_norm(one_k[...], kg, cos_ref[1], sin_ref[1])
    xk2, inv2, k2 = forward_norm(jnp.where(take, two_k[...], own_k[...]), kg, cos2, sin2)
    k_wide = jnp.concatenate([k0, k2], axis=1)
    v_wide = jnp.concatenate([v0, jnp.where(take, two_v[...], v0)], axis=1)

    bias_a = jnp.concatenate([bias_ref[0]] * GROUP, axis=1)
    bias_b = jnp.concatenate([bias_ref[1]] * GROUP, axis=1)
    s_a = dot(k1, q, NT) * scale + bias_a
    s_b = dot(k_wide, q_wide, NT) * scale + bias_b
    top = jnp.maximum(jnp.max(s_a, axis=0, keepdims=True), jnp.max(s_b, axis=0, keepdims=True))
    w_a, w_b = jnp.exp(s_a - top), jnp.exp(s_b - top)
    inv_sum = 1.0 / (jnp.sum(w_a, axis=0, keepdims=True) + jnp.sum(w_b, axis=0, keepdims=True))
    p_a, p_b = w_a * inv_sum, w_b * inv_sum
    dp_a = dot(v1, do, NT)
    dp_b = dot(v_wide, do_wide, NT)
    delta = jnp.sum(p_a * dp_a, axis=0, keepdims=True) + jnp.sum(p_b * dp_b, axis=0, keepdims=True)
    ds_a = (p_a * (dp_a - delta) * scale).astype(jnp.bfloat16)
    ds_b = (p_b * (dp_b - delta) * scale).astype(jnp.bfloat16)

    dv1 = dot(p_a.astype(jnp.bfloat16), do, NN)
    dv_wide = dot(p_b.astype(jnp.bfloat16), do_wide, NN)
    dk1 = dot(ds_a, q, NN)
    dk_wide = dot(ds_b, q_wide, NN)
    dk0, dk2 = dk_wide[:, :HEAD_DIM], dk_wide[:, HEAD_DIM:]
    dv0, dv2 = dv_wide[:, :HEAD_DIM], dv_wide[:, HEAD_DIM:]

    dq_wide = dot(ds_b, k_wide, TN)
    dq = dot(ds_a, k1, TN) + jnp.where(late4, dq_wide[:, HEAD_DIM:], dq_wide[:, :HEAD_DIM])
    dq = dq.astype(jnp.bfloat16).astype(jnp.float32)
    dy = unrotate(dq, cos4, sin4)
    e = dy * qg
    mean = jnp.mean(e * x, axis=-1, keepdims=True)
    dx = (inv_q * (e - x * (inv_q * inv_q * mean))).astype(jnp.bfloat16)
    for h in range(GROUP):
        dq_ref[:, h * HEAD_DIM:(h + 1) * HEAD_DIM] = dx[h * ROWS:(h + 1) * ROWS]

    gk = unrotate(dk0, cos0, sin0) * (xk0 * inv0)
    gk = gk + unrotate(dk1, cos_ref[1], sin_ref[1]) * (xk1 * inv1)
    gk = gk + unrotate(dk2, cos2, sin2) * (xk2 * inv2)
    parts = (fold8(dy * (x * inv_q)), fold8(gk))

    @pl.when(step == 0)
    def _():
        total_ref[0], total_ref[1] = parts

    @pl.when(step > 0)
    def _():
        total_ref[0] += parts[0]
        total_ref[1] += parts[1]

    @pl.when(step == pl.num_programs(0) - 1)
    def _():
        gains_ref[...] = jnp.broadcast_to(jnp.sum(total_ref[...], axis=1)[None], gains_ref.shape)

    ret1_ref[:, :HEAD_DIM] = dk1.astype(jnp.bfloat16)
    ret1_ref[:, HEAD_DIM:] = dv1.astype(jnp.bfloat16)
    ret2_ref[:, :HEAD_DIM] = jnp.where(take, dk2, 0.0).astype(jnp.bfloat16)
    ret2_ref[:, HEAD_DIM:] = jnp.where(take, dv2, 0.0).astype(jnp.bfloat16)
    keep_ref[:, :HEAD_DIM] = dk0 + jnp.where(take, 0.0, dk2)
    keep_ref[:, HEAD_DIM:] = dv0 + jnp.where(take, 0.0, dv2)


def blocks(width, index):
    return pl.BlockSpec((ROWS, width), lambda g: (0, index(g)))


def fixed(a):
    return pl.BlockSpec(a.shape, lambda g: (0,) * a.ndim)


def attend(q, do, own, one, two, tables, peers):
    wide, pair = GROUP * HEAD_DIM, 2 * HEAD_DIM
    here = lambda g: g
    beside = lambda g: g + KV_HEADS
    kv = [blocks(HEAD_DIM, here), blocks(HEAD_DIM, beside)]
    return pl.pallas_call(
        attend_kernel,
        grid=(KV_HEADS,),
        in_specs=[blocks(wide, here), blocks(wide, here)] + kv * 3 + [fixed(t) for t in tables],
        out_specs=[
            blocks(wide, here), blocks(pair, here), blocks(pair, here), blocks(pair, here),
            pl.BlockSpec((peers, 2, HEAD_DIM), lambda g: (0, 0, 0)),
        ],
        out_shape=[
            jax.ShapeDtypeStruct((ROWS, KV_HEADS * wide), jnp.bfloat16),
            jax.ShapeDtypeStruct((ROWS, KV_HEADS * pair), jnp.bfloat16),
            jax.ShapeDtypeStruct((ROWS, KV_HEADS * pair), jnp.bfloat16),
            jax.ShapeDtypeStruct((ROWS, KV_HEADS * pair), jnp.float32),
            jax.ShapeDtypeStruct((peers, 2, HEAD_DIM), jnp.float32),
        ],
        scratch_shapes=[pltpu.VMEM((2, 8, HEAD_DIM), jnp.float32)],
        compiler_params=pltpu.CompilerParams(vmem_limit_bytes=40 * 1024 * 1024),
        name="attend",
    )(q, do, own, own, one, one, two, two, *tables)


def finish_kernel(k_ref, keep_ref, one_ref, two_ref, cos_ref, sin_ref, gain_ref, dk_ref, dv_ref):
    gain = jnp.sum(gain_ref[...], axis=0)[1:2]
    total = keep_ref[...] + one_ref[...].astype(jnp.float32) + two_ref[...].astype(jnp.float32)
    for h in range(k_ref.shape[1] // HEAD_DIM):
        at = slice(h * HEAD_DIM, (h + 1) * HEAD_DIM)
        x = k_ref[:, at].astype(jnp.float32)
        inverse = lax.rsqrt(jnp.mean(x * x, axis=-1, keepdims=True) + norm_epsilon)
        dk = total[:, 2 * h * HEAD_DIM:(2 * h + 1) * HEAD_DIM].astype(jnp.bfloat16).astype(jnp.float32)
        e = unrotate(dk, cos_ref[0], sin_ref[0]) * gain
        mean = jnp.mean(e * x, axis=-1, keepdims=True)
        dk_ref[:, at] = (inverse * (e - x * (inverse * inverse * mean))).astype(jnp.bfloat16)
        dv_ref[:, at] = total[:, (2 * h + 1) * HEAD_DIM:(2 * h + 2) * HEAD_DIM].astype(jnp.bfloat16)


def finish(k, keep, one, two, cosine, sine, gain):
    steps = max(KV_HEADS // 2, 1)
    width = KV_HEADS * HEAD_DIM // steps
    here = lambda g: g
    out = jax.ShapeDtypeStruct((ROWS, KV_HEADS * HEAD_DIM), jnp.bfloat16)
    return pl.pallas_call(
        finish_kernel,
        grid=(steps,),
        in_specs=[blocks(width, here)] + [blocks(2 * width, here)] * 3 + [fixed(t) for t in (cosine, sine, gain)],
        out_specs=[blocks(width, here)] * 2,
        out_shape=[out, out],
        compiler_params=pltpu.CompilerParams(vmem_limit_bytes=40 * 1024 * 1024),
        name="finish",
    )(k, keep, one, two, cosine, sine, gain)


def rotary_tables(base):
    positions = base + jnp.arange(ROWS, dtype=jnp.int32)
    positions = positions[None, :] - ROWS * jnp.arange(3, dtype=jnp.int32)[:, None]
    freqs = rope_base ** (-(jnp.arange(HALF, dtype=jnp.float32) * 2.0 / HEAD_DIM))
    angles = positions.astype(jnp.float32)[:, :, None] * freqs
    cosine, sine = jnp.cos(angles), jnp.sin(angles)
    return jnp.concatenate([cosine, cosine], axis=2), jnp.concatenate([-sine, sine], axis=2)


AXES = ("seq", "fsdp")


def device_at(y, z, x, core):
    return ((y % 4 * 4 + x) * 2 + core) * 16 + y // 4 * 8 + z


def gain_groups():
    return [
        [device_at(a, z, x, c) for z in range(8)] + [device_at(4 + (a + 2) % 4, z, x, c) for z in range(8)]
        for a in range(4) for x in range(4) for c in range(2)
    ]


def plane_groups():
    return [[device_at(y, z, x, c) for z in range(8) for x in range(4) for c in range(2)] for y in range(8)]


def column_groups():
    return [[device_at(y, z, x, c) for y in range(8)] for z in range(8) for x in range(4) for c in range(2)]


def swap(rows, groups):
    return lax.all_to_all(rows, AXES, 0, 0, axis_index_groups=groups, tiled=True)


def local(query_raw, key_raw, value_proj, out_grad, query_gain, key_gain, turn_lengths):
    me, shard = lax.axis_index("seq"), lax.axis_index("fsdp")
    seq, shards = lax.axis_size("seq"), lax.axis_size("fsdp")
    base = me * ROWS

    own = jnp.concatenate([key_raw[0], value_proj[0]], axis=1)
    two = lax.ppermute(own, "seq", [(i, i + 2) for i in range(seq - 2)])
    one = lax.ppermute(own, "seq", [(i, i + 1) for i in range(seq - 1)])

    gain = jnp.tile(jnp.stack([query_gain, key_gain]), (1, shards))
    mine = jnp.arange(HEAD_DIM, dtype=jnp.int32) // query_gain.shape[0] == shard
    gain = jnp.where(mine, gain, 0.0)
    gain = swap(jnp.broadcast_to(gain[None], (shards, 2, HEAD_DIM)), gain_groups())

    cosine, sine = rotary_tables(base)
    bias, late, take = block_tables(turn_lengths[0], base[None])
    tables = (cosine, sine, bias, late, take, gain)
    q_grad, ret1, ret2, keep, parts = attend(query_raw[0], out_grad[0], own, one, two, tables, 64)

    back2 = lax.ppermute(ret2, "seq", [(i + 2, i) for i in range(seq - 2)])
    back1 = lax.ppermute(ret1, "seq", [(i + 1, i) for i in range(seq - 1)])

    part = jnp.sum(swap(parts, plane_groups()), axis=0)
    total = jnp.sum(swap(jnp.broadcast_to(part[None], (8, 2, HEAD_DIM)), column_groups()), axis=0)
    shard_rows = total.reshape(2, shards, HEAD_DIM // shards)
    gain_grad = lax.dynamic_slice_in_dim(shard_rows, shard, 1, axis=1)

    k_grad, v_grad = finish(key_raw[0], keep, back1, back2, cosine, sine, gain)
    return q_grad[None], k_grad[None], v_grad[None], gain_grad[0, 0], gain_grad[1, 0]


def solution(mesh):
    return jax.shard_map(
        local,
        mesh=mesh,
        in_specs=(
            P("fsdp", "seq", None),
            P("fsdp", "seq", None),
            P("fsdp", "seq", None),
            P("fsdp", "seq", None),
            P("fsdp"),
            P("fsdp"),
            P("fsdp", None),
        ),
        out_specs=(
            P("fsdp", "seq", None),
            P("fsdp", "seq", None),
            P("fsdp", "seq", None),
            P("fsdp"),
            P("fsdp"),
        ),
        check_vma=False,
    )
```

```python
import jax
import jax.numpy as jnp
import numpy as np
from jax import lax
from jax.experimental import pallas as pl
from jax.experimental.pallas import tpu as pltpu
from jax.sharding import PartitionSpec as P

HEADS = 32
KV_HEADS = 8
GROUP = HEADS // KV_HEADS
HEAD_DIM = 128
HALF = HEAD_DIM // 2
ROWS = 128

norm_epsilon = 1e-06
rope_base = 1000000.0
MASKED = -1e30
LOG2E = 1.4426950408889634
STEP_HEADS = 4
VMEM = 24 * 1024 * 1024

NT = (((1,), (1,)), ((), ()))
NN = (((1,), (0,)), ((), ()))
TN = (((0,), (0,)), ((), ()))


def dot(a, b, dims):
    return lax.dot_general(a, b, dims, preferred_element_type=jnp.float32)


def roll_half(x):
    return pltpu.roll(x, HALF, axis=1)


def forward_norm(raw, gain, cosine, sine):
    x = raw.astype(jnp.float32)
    inverse = lax.rsqrt(jnp.mean(x * x, axis=-1, keepdims=True) + norm_epsilon)
    y = x * inverse * gain
    return x, inverse, (y * cosine + roll_half(y) * sine).astype(jnp.bfloat16)


def unrotate(grad, cosine, sine):
    return grad * cosine - roll_half(grad) * sine


def swap_halves(x):
    return jnp.concatenate([x[HALF:], x[:HALF]], axis=0)


def beside_heads(x):
    return jnp.concatenate([x[h * HEAD_DIM:(h + 1) * HEAD_DIM] for h in range(GROUP)], axis=1)


def over_heads(x):
    return jnp.concatenate([x[:, h * ROWS:(h + 1) * ROWS] for h in range(GROUP)], axis=0)


def fold8(x):
    return jnp.sum(x.reshape(x.shape[0] // 8, 8, x.shape[1]), axis=0)


def stack_heads(x):
    return jnp.concatenate([x[:, h * HEAD_DIM:(h + 1) * HEAD_DIM] for h in range(GROUP)], axis=0)


def table_kernel(len_ref, place_ref, freq_ref, table_ref, late_ref):
    shape = (ROWS, ROWS)
    base = place_ref[0]
    row = lax.broadcasted_iota(jnp.int32, shape, 0)
    lane = lax.broadcasted_iota(jnp.int32, shape, 1)
    for back in range(3):
        angles = (base - back * ROWS + row).astype(jnp.float32) * freq_ref[...]
        cosine, sine = jnp.cos(angles), jnp.sin(angles)
        sine = jnp.where(lane < HALF, -sine, sine)
        table_ref[back], table_ref[3 + back] = cosine, sine
        if back == 0:
            table_ref[6], table_ref[7] = cosine.T, sine.T

    here = lax.broadcasted_iota(jnp.int32, (8, ROWS), 1)
    first = jnp.zeros((8, ROWS), jnp.int32) - base
    end = -base
    for k in range(len_ref.shape[0] - 1):
        end = end + len_ref[k]
        first = jnp.where(here >= end, end, first)
    first = jnp.concatenate([first] * (ROWS // 8), axis=0)
    table_ref[8] = jnp.where(row >= first + ROWS, 0.0, MASKED)
    own = (row <= lane) & (row >= first)
    table_ref[9] = jnp.where(own | (row >= first + 2 * ROWS), 0.0, MASKED)
    head = jnp.broadcast_to(first[:, 0:1], shape)
    table_ref[10] = jnp.where(row >= head + 2 * ROWS, 1.0, 0.0)
    late = jnp.where(first < -ROWS, 1.0, 0.0)
    late_ref[0] = late.T.astype(jnp.bfloat16)
    late_ref[1] = (1.0 - late).T.astype(jnp.bfloat16)
    late_ref[2] = late.astype(jnp.bfloat16)
    late_ref[3] = (1.0 - late).astype(jnp.bfloat16)


SMEM_IN = pl.BlockSpec(memory_space=pltpu.SMEM)
VMEM_IN = pl.BlockSpec(memory_space=pltpu.VMEM)
HBM_IN = pl.BlockSpec(memory_space=pltpu.HBM)


def in_hbm(*arrays):
    return [pltpu.with_memory_space_constraint(a, pltpu.HBM) for a in arrays]


def block_tables(lengths, place):
    half = rope_base ** (-np.arange(HALF) * 2.0 / HEAD_DIM)
    freqs = jnp.asarray(np.concatenate([half, half])[None], jnp.float32)
    return pl.pallas_call(
        table_kernel,
        in_specs=[SMEM_IN, SMEM_IN, VMEM_IN],
        out_specs=[VMEM_IN] * 2,
        out_shape=[
            pltpu.VMEM((11, ROWS, ROWS), jnp.float32),
            pltpu.VMEM((4, ROWS, ROWS), jnp.bfloat16),
        ],
        compiler_params=pltpu.CompilerParams(vmem_limit_bytes=VMEM),
        name="tables",
    )(lengths, place, freqs)


def pack_kernel(k_ref, v_ref, qg_in, kg_in, shard_ref, own_ref, gain_ref, qg_ref, kg_ref, sems):
    copies = [
        pltpu.make_async_copy(
            ref.at[:, pl.ds(h * HEAD_DIM, HEAD_DIM)],
            own_ref.at[:, pl.ds((2 * h + n) * HEAD_DIM, HEAD_DIM)],
            sems.at[2 * h + n],
        )
        for h in range(KV_HEADS) for n, ref in enumerate((k_ref, v_ref))
    ]
    gains = [
        pltpu.make_async_copy(source, target, sems.at[2 * KV_HEADS + n])
        for n, (source, target) in enumerate(((qg_in, qg_ref), (kg_in, kg_ref)))
    ]
    for copy in gains + copies:
        copy.start()
    for copy in gains:
        copy.wait()
    width = qg_ref.shape[0]
    lane = lax.broadcasted_iota(jnp.int32, (2, HEAD_DIM), 1) - shard_ref[0] * width
    row = lax.broadcasted_iota(jnp.int32, (2, HEAD_DIM), 0)
    both = jnp.zeros((2, HEAD_DIM), jnp.float32)
    for i in range(width):
        both = jnp.where(lane == i, jnp.where(row == 0, qg_ref[i], kg_ref[i]), both)
    gain_ref[...] = jnp.broadcast_to(both[None], gain_ref.shape)
    for copy in copies:
        copy.wait()


def pack(k, v, q_gain, k_gain, shard, shards):
    return pl.pallas_call(
        pack_kernel,
        in_specs=[HBM_IN] * 4 + [SMEM_IN],
        out_specs=[VMEM_IN, VMEM_IN],
        out_shape=[
            pltpu.VMEM((ROWS, 2 * KV_HEADS * HEAD_DIM), jnp.bfloat16),
            pltpu.VMEM((shards, 2, HEAD_DIM), jnp.float32),
        ],
        scratch_shapes=[
            pltpu.SMEM(q_gain.shape, jnp.float32),
            pltpu.SMEM(k_gain.shape, jnp.float32),
            pltpu.SemaphoreType.DMA((2 * KV_HEADS + 2,)),
        ],
        compiler_params=pltpu.CompilerParams(vmem_limit_bytes=VMEM),
        name="pack",
    )(*in_hbm(k, v, q_gain, k_gain), shard)


def forward_keys(raw, gain, cosine, sine):
    x = raw.astype(jnp.float32)
    unit = x * lax.rsqrt(jnp.mean(x * x, axis=-1, keepdims=True) + norm_epsilon)
    straight, across = unit * cosine, roll_half(unit) * sine
    return straight, across, (straight * gain + across * roll_half(gain)).astype(jnp.bfloat16)


def over(a, b):
    return jnp.concatenate([a, b], axis=0)


def beside(a, b):
    return jnp.concatenate([a, b], axis=1)


def wide(a):
    return jnp.concatenate([a] * GROUP, axis=1)


def tall(a):
    return jnp.concatenate([a] * GROUP, axis=0)


def attend_kernel(
    q_in, do_in, own_ref, one_ref, two_ref, table_ref, late_ref, gain_ref,
    dq_out, ret1_out, ret2_out, keep_ref, gains_ref, q_ref, do_ref, dq_ref, ret1_ref, ret2_ref, q_total, k_total, in_sems, sems,
):
    group, pair = GROUP * HEAD_DIM, 2 * HEAD_DIM

    def fetch(step):
        width = STEP_HEADS * group
        at = pl.ds(pl.multiple_of(step * width, HEAD_DIM), width)
        return [
            pltpu.make_async_copy(source.at[:, at], target.at[:, at], in_sems.at[n, step])
            for n, (source, target) in enumerate(((q_in, q_ref), (do_in, do_ref)))
        ]

    for step in range(KV_HEADS // STEP_HEADS):
        for copy in fetch(step):
            copy.start()
    gain = jnp.sum(gain_ref[...], axis=0)
    kg = gain[1:2]
    qgt = jnp.broadcast_to(gain[0:1], (HEAD_DIM, HEAD_DIM)).T
    cost, sint = table_ref[6], table_ref[7]
    turn, cross, uncross = wide(qgt * cost), wide(swap_halves(qgt) * sint), wide(qgt * sint)
    late, on_time = tall(late_ref[0]), tall(late_ref[1])
    latet, on_timet = wide(late_ref[2]), wide(late_ref[3])
    take = table_ref[10] > 0.0
    cos0, sin0 = table_ref[0], table_ref[3]
    cos1, sin1 = table_ref[1], table_ref[4]
    cos2 = jnp.where(take, table_ref[2], cos0)
    sin2 = jnp.where(take, table_ref[5], sin0)
    bias = over(wide(table_ref[8]), wide(table_ref[9]))
    q_total[...] = jnp.zeros_like(q_total)
    k_total[...] = jnp.zeros_like(k_total)

    def out(step):
        copies = []
        for n, (source, target) in enumerate(((dq_ref, dq_out), (ret1_ref, ret1_out), (ret2_ref, ret2_out))):
            width = STEP_HEADS * (group if n == 0 else pair)
            at = pl.ds(pl.multiple_of(step * width, HEAD_DIM), width)
            copies.append(pltpu.make_async_copy(source.at[:, at], target.at[:, at], sems.at[n, step]))
        return copies

    def one_head(head):
        heads = pl.ds(pl.multiple_of(head * group, group), group)
        at_k = pl.ds(pl.multiple_of(head * pair, HEAD_DIM), HEAD_DIM)
        at_v = pl.ds(pl.multiple_of(head * pair + HEAD_DIM, HEAD_DIM), HEAD_DIM)
        xt = beside_heads(q_ref[:, heads].T).astype(jnp.float32)
        inv_q = lax.rsqrt(jnp.mean(xt * xt, axis=0, keepdims=True) + norm_epsilon)
        qt = ((xt * turn + swap_halves(xt) * cross) * inv_q).astype(jnp.bfloat16)
        q = jnp.concatenate([qt[:, h * ROWS:(h + 1) * ROWS].T for h in range(GROUP)], axis=0)
        do = stack_heads(do_ref[:, heads])
        dot_ = beside_heads(do_ref[:, heads].T)
        qt_wide = over(qt * on_timet, qt * latet)
        dot_wide = over(dot_ * on_timet, dot_ * latet)
        q_wide = beside(q * on_time, q * late)
        do_wide = beside(do * on_time, do * late)

        v0, v1 = own_ref[:, at_v], one_ref[:, at_v]
        v2 = jnp.where(take, two_ref[:, at_v], v0)
        straight0, across0, k0 = forward_keys(own_ref[:, at_k], kg, cos0, sin0)
        straight1, across1, k1 = forward_keys(one_ref[:, at_k], kg, cos1, sin1)
        straight2, across2, k2 = forward_keys(jnp.where(take, two_ref[:, at_k], own_ref[:, at_k]), kg, cos2, sin2)
        k_all = over(beside(k1, k1), beside(k0, k2))
        v_all = over(beside(v1, v1), beside(v0, v2))
        k1t = k1.T
        kt_all = over(beside(k1t, k0.T), beside(k1t, k2.T))

        s = dot(k_all, qt_wide, NN) * (HEAD_DIM ** (-0.5) * LOG2E) + bias
        w = jnp.exp2(s - jnp.max(s, axis=0, keepdims=True))
        p = w * (1.0 / jnp.sum(w, axis=0, keepdims=True))
        dp = dot(v_all, dot_wide, NN)
        delta = jnp.sum(p * dp, axis=0, keepdims=True)
        ds = (p * (dp - delta) * (HEAD_DIM ** (-0.5))).astype(jnp.bfloat16)

        dv = dot(p.astype(jnp.bfloat16), do_wide, NN)
        dk = dot(ds, q_wide, NN)
        dk1, dv1 = dk[:ROWS, :HEAD_DIM] + dk[:ROWS, HEAD_DIM:], dv[:ROWS, :HEAD_DIM] + dv[:ROWS, HEAD_DIM:]
        dk0, dk2 = dk[ROWS:, :HEAD_DIM], dk[ROWS:, HEAD_DIM:]
        dv0, dv2 = dv[ROWS:, :HEAD_DIM], dv[ROWS:, HEAD_DIM:]

        dqt = dot(kt_all, ds, NN)
        dqt = jnp.where(latet > 0.0, dqt[HEAD_DIM:], dqt[:HEAD_DIM])
        dqt = dqt.astype(jnp.bfloat16).astype(jnp.float32)
        et = dqt * turn - swap_halves(dqt) * uncross
        ext = et * xt
        mean = jnp.mean(ext, axis=0, keepdims=True)
        dxt = (et * inv_q - xt * (inv_q * inv_q * inv_q * mean)).astype(jnp.bfloat16)
        dq_ref[:, heads] = over_heads(dxt).T
        ext = ext * inv_q
        q_total[...] += sum(ext[:, h * ROWS:(h + 1) * ROWS] for h in range(GROUP))
        k_total[0] += fold8(dk0 * straight0 + dk1 * straight1 + dk2 * straight2)
        k_total[1] += fold8(dk0 * across0 + dk1 * across1 + dk2 * across2)

        ret1_ref[:, at_k] = dk1.astype(jnp.bfloat16)
        ret1_ref[:, at_v] = dv1.astype(jnp.bfloat16)
        ret2_ref[:, at_k] = jnp.where(take, dk2, 0.0).astype(jnp.bfloat16)
        ret2_ref[:, at_v] = jnp.where(take, dv2, 0.0).astype(jnp.bfloat16)
        keep_ref[:, at_k] = dk0 + jnp.where(take, 0.0, dk2)
        keep_ref[:, at_v] = dv0 + jnp.where(take, 0.0, dv2)

    @pl.loop(0, KV_HEADS // STEP_HEADS)
    def _(step):
        for copy in fetch(step):
            copy.wait()
        for n in range(STEP_HEADS):
            one_head(step * STEP_HEADS + n)
        for copy in out(step):
            copy.start()

    q_gain_grad = jnp.sum(q_total[...].T, axis=0, keepdims=True) / gain[0:1]
    k_gain_grad = jnp.sum(k_total[0] + roll_half(k_total[1]), axis=0, keepdims=True)
    gains_ref[...] = jnp.broadcast_to(over(q_gain_grad, k_gain_grad)[None], gains_ref.shape)

    @pl.loop(0, KV_HEADS // STEP_HEADS)
    def _(step):
        for copy in out(step):
            copy.wait()


def attend(q, do, own, one, two, tables, peers):
    pair = (ROWS, 2 * KV_HEADS * HEAD_DIM)
    return pl.pallas_call(
        attend_kernel,
        in_specs=[HBM_IN] * 2 + [VMEM_IN] * 6,
        out_specs=[HBM_IN] * 3 + [VMEM_IN] * 2,
        out_shape=[
            pltpu.HBM(q.shape, jnp.bfloat16),
            pltpu.HBM(pair, jnp.bfloat16),
            pltpu.HBM(pair, jnp.bfloat16),
            pltpu.VMEM(pair, jnp.float32),
            pltpu.VMEM((peers, 2, HEAD_DIM), jnp.float32),
        ],
        scratch_shapes=[
            pltpu.VMEM(q.shape, jnp.bfloat16),
            pltpu.VMEM(q.shape, jnp.bfloat16),
            pltpu.VMEM(q.shape, jnp.bfloat16),
            pltpu.VMEM(pair, jnp.bfloat16),
            pltpu.VMEM(pair, jnp.bfloat16),
            pltpu.VMEM((HEAD_DIM, HEAD_DIM), jnp.float32),
            pltpu.VMEM((2, 8, HEAD_DIM), jnp.float32),
            pltpu.SemaphoreType.DMA((2, KV_HEADS // STEP_HEADS)),
            pltpu.SemaphoreType.DMA((3, KV_HEADS // STEP_HEADS)),
        ],
        compiler_params=pltpu.CompilerParams(vmem_limit_bytes=VMEM),
        name="attend",
    )(*in_hbm(q, do), own, one, two, *tables)


def finish_kernel(own_ref, keep_ref, one_ref, two_ref, table_ref, gain_ref, dk_ref, dv_ref, stage, sems):
    gain = jnp.sum(gain_ref[...], axis=0)[1:2]
    copies = []
    for h in range(KV_HEADS):
        at_k, at_v = pl.ds(2 * h * HEAD_DIM, HEAD_DIM), pl.ds((2 * h + 1) * HEAD_DIM, HEAD_DIM)
        dk, dv = (keep_ref[:, at] + one_ref[:, at] + two_ref[:, at] for at in (at_k, at_v))
        x = own_ref[:, at_k].astype(jnp.float32)
        inverse = lax.rsqrt(jnp.mean(x * x, axis=-1, keepdims=True) + norm_epsilon)
        dk = dk.astype(jnp.bfloat16).astype(jnp.float32)
        e = unrotate(dk, table_ref[0], table_ref[3]) * gain
        mean = jnp.mean(e * x, axis=-1, keepdims=True)
        stage[0, h] = (inverse * (e - x * (inverse * inverse * mean))).astype(jnp.bfloat16)
        stage[1, h] = dv.astype(jnp.bfloat16)
        for n, ref in enumerate((dk_ref, dv_ref)):
            at = pl.ds(h * HEAD_DIM, HEAD_DIM)
            copies.append(pltpu.make_async_copy(stage.at[n, h], ref.at[:, at], sems.at[n, h]))
            copies[-1].start()
    for copy in copies:
        copy.wait()


def finish(own, keep, one, two, table, gain):
    out = jax.ShapeDtypeStruct((ROWS, KV_HEADS * HEAD_DIM), jnp.bfloat16)
    return pl.pallas_call(
        finish_kernel,
        in_specs=[VMEM_IN] * 6,
        out_specs=[HBM_IN] * 2,
        out_shape=[out, out],
        scratch_shapes=[
            pltpu.VMEM((2, KV_HEADS, ROWS, HEAD_DIM), jnp.bfloat16),
            pltpu.SemaphoreType.DMA((2, KV_HEADS)),
        ],
        compiler_params=pltpu.CompilerParams(vmem_limit_bytes=VMEM),
        name="finish",
    )(own, keep, one, two, table, gain)


AXES = ("seq", "fsdp")


def device_at(y, z, x, core):
    return ((y % 4 * 4 + x) * 2 + core) * 16 + y // 4 * 8 + z


def gain_groups():
    return [
        [device_at(a, z, x, c) for z in range(8)] + [device_at(4 + (a + 2) % 4, z, x, c) for z in range(8)]
        for a in range(4) for x in range(4) for c in range(2)
    ]


def plane_groups():
    return [[device_at(y, z, x, c) for z in range(8) for x in range(4) for c in range(2)] for y in range(8)]


def column_groups():
    return [[device_at(y, z, x, c) for y in range(8)] for z in range(8) for x in range(4) for c in range(2)]


def swap(rows, groups):
    return lax.all_to_all(rows, AXES, 0, 0, axis_index_groups=groups, tiled=True)


def local(query_raw, key_raw, value_proj, out_grad, query_gain, key_gain, turn_lengths):
    me, shard = lax.axis_index("seq"), lax.axis_index("fsdp")
    seq, shards = lax.axis_size("seq"), lax.axis_size("fsdp")
    base = me * ROWS

    own, gain = pack(key_raw[0], value_proj[0], query_gain, key_gain, shard[None], shards)
    table, late = block_tables(turn_lengths[0], base[None])
    two = lax.ppermute(own, "seq", [(i, i + 2) for i in range(seq - 2)])
    gain = swap(gain, gain_groups())
    one, gain, table = lax.optimization_barrier((jnp.where(me % 2 == 1, two, own), gain, table))
    one = lax.ppermute(one, "seq", [(i, i ^ 1) for i in range(seq)])
    q_grad, ret1, ret2, keep, parts = attend(query_raw[0], out_grad[0], own, one, two, (table, late, gain), 64)

    back2 = lax.ppermute(ret2, "seq", [(i + 2, i) for i in range(seq - 2)])
    part = jnp.sum(swap(parts, plane_groups()), axis=0)
    ret1, part = lax.optimization_barrier((ret1, part))
    back1 = lax.ppermute(ret1, "seq", [(i + 1, i) for i in range(seq - 1)])
    total = swap(jnp.broadcast_to(part[None], (8, 2, HEAD_DIM)), column_groups())
    k_grad, v_grad = finish(own, keep, back1, back2, table, gain)
    total, k_grad, v_grad = lax.optimization_barrier((total, k_grad, v_grad))
    total = jnp.sum(total, axis=0)
    shard_rows = total.reshape(2, shards, HEAD_DIM // shards)
    gain_grad = lax.dynamic_slice_in_dim(shard_rows, shard, 1, axis=1)

    return q_grad[None], k_grad[None], v_grad[None], gain_grad[0, 0], gain_grad[1, 0]


def solution(mesh):
    return jax.shard_map(
        local,
        mesh=mesh,
        in_specs=(
            P("fsdp", "seq", None),
            P("fsdp", "seq", None),
            P("fsdp", "seq", None),
            P("fsdp", "seq", None),
            P("fsdp"),
            P("fsdp"),
            P("fsdp", None),
        ),
        out_specs=(
            P("fsdp", "seq", None),
            P("fsdp", "seq", None),
            P("fsdp", "seq", None),
            P("fsdp"),
            P("fsdp"),
        ),
        check_vma=False,
    )
```

```python
import jax
import jax.numpy as jnp
import numpy as np
from jax import lax
from jax.experimental import pallas as pl
from jax.experimental.pallas import tpu as pltpu
from jax.sharding import PartitionSpec as P

HEADS = 32
KV_HEADS = 8
GROUP = HEADS // KV_HEADS
HEAD_DIM = 128
HALF = HEAD_DIM // 2
ROWS = 128

norm_epsilon = 1e-06
rope_base = 1000000.0
MASKED = -1e30
LOG2E = 1.4426950408889634
OUT_HEADS = 2
FIRST_HEADS = 2
VMEM = 24 * 1024 * 1024

NT = (((1,), (1,)), ((), ()))
NN = (((1,), (0,)), ((), ()))
TN = (((0,), (0,)), ((), ()))


def dot(a, b, dims):
    return lax.dot_general(a, b, dims, preferred_element_type=jnp.float32)


def roll_half(x):
    return pltpu.roll(x, HALF, axis=1)


def forward_norm(raw, gain, cosine, sine):
    x = raw.astype(jnp.float32)
    inverse = lax.rsqrt(jnp.mean(x * x, axis=-1, keepdims=True) + norm_epsilon)
    y = x * inverse * gain
    return x, inverse, (y * cosine + roll_half(y) * sine).astype(jnp.bfloat16)


def unrotate(grad, cosine, sine):
    return grad * cosine - roll_half(grad) * sine


def swap_halves(x):
    return jnp.concatenate([x[HALF:], x[:HALF]], axis=0)


def beside_heads(x):
    return jnp.concatenate([x[h * HEAD_DIM:(h + 1) * HEAD_DIM] for h in range(GROUP)], axis=1)


def over_heads(x):
    return jnp.concatenate([x[:, h * ROWS:(h + 1) * ROWS] for h in range(GROUP)], axis=0)


def fold8(x):
    return jnp.sum(x.reshape(x.shape[0] // 8, 8, x.shape[1]), axis=0)


def stack_heads(x):
    return jnp.concatenate([x[:, h * HEAD_DIM:(h + 1) * HEAD_DIM] for h in range(GROUP)], axis=0)


def table_kernel(len_ref, place_ref, freq_ref, q_in, do_in, table_ref, row_ref, q_ref, do_ref, sems):
    copies = [
        pltpu.make_async_copy(source.at[:, pl.ds(0, target.shape[1])], target, sems.at[n])
        for n, (source, target) in enumerate(((q_in, q_ref), (do_in, do_ref)))
    ]
    for copy in copies:
        copy.start()
    base = place_ref[0]
    freqs = freq_ref[...]
    token = lax.broadcasted_iota(jnp.int32, (ROWS, HEAD_DIM), 0) + base
    angles = token.astype(jnp.float32) * freqs
    table_ref[0] = jnp.cos(angles)
    table_ref[1] = signed(jnp.sin(angles))

    here = lax.broadcasted_iota(jnp.int32, (8, ROWS), 1)
    first = jnp.zeros((8, ROWS), jnp.int32) - base
    end = -base
    for k in range(len_ref.shape[0] - 1):
        end = end + len_ref[k]
        first = jnp.where(here >= end, end, first)
    row_ref[0] = first.astype(jnp.float32)
    for n in (1, 2):
        angle = jnp.broadcast_to(freqs * float(n * ROWS), (8, HEAD_DIM))
        row_ref[2 * n - 1] = jnp.cos(angle)
        row_ref[2 * n] = signed(jnp.sin(angle))
    for copy in copies:
        copy.wait()


def signed(sine):
    lane = lax.broadcasted_iota(jnp.int32, sine.shape, 1)
    return jnp.where(lane < HALF, -sine, sine)


SMEM_IN = pl.BlockSpec(memory_space=pltpu.SMEM)
VMEM_IN = pl.BlockSpec(memory_space=pltpu.VMEM)
HBM_IN = pl.BlockSpec(memory_space=pltpu.HBM)


def in_hbm(*arrays):
    return [pltpu.with_memory_space_constraint(a, pltpu.HBM) for a in arrays]


def block_tables(lengths, place, q, do):
    half = rope_base ** (-np.arange(HALF) * 2.0 / HEAD_DIM)
    freqs = jnp.asarray(np.concatenate([half, half])[None], jnp.float32)
    return pl.pallas_call(
        table_kernel,
        in_specs=[SMEM_IN, SMEM_IN, VMEM_IN, HBM_IN, HBM_IN],
        out_specs=[VMEM_IN] * 4,
        out_shape=[
            pltpu.VMEM((2, ROWS, HEAD_DIM), jnp.float32),
            pltpu.VMEM((5, 8, HEAD_DIM), jnp.float32),
            pltpu.VMEM((ROWS, FIRST_HEADS * GROUP * HEAD_DIM), q.dtype),
            pltpu.VMEM((ROWS, FIRST_HEADS * GROUP * HEAD_DIM), q.dtype),
        ],
        scratch_shapes=[pltpu.SemaphoreType.DMA((2,))],
        compiler_params=pltpu.CompilerParams(vmem_limit_bytes=VMEM),
        name="tables",
    )(lengths, place, freqs, *in_hbm(q, do))


def pack_kernel(k_ref, v_ref, qg_in, kg_in, shard_ref, own_ref, gain_ref, qg_ref, kg_ref, sems):
    copies = [
        pltpu.make_async_copy(
            ref.at[:, pl.ds(h * HEAD_DIM, HEAD_DIM)],
            own_ref.at[:, pl.ds((2 * h + n) * HEAD_DIM, HEAD_DIM)],
            sems.at[2 * h + n],
        )
        for h in range(KV_HEADS) for n, ref in enumerate((k_ref, v_ref))
    ]
    gains = [
        pltpu.make_async_copy(source, target, sems.at[2 * KV_HEADS + n])
        for n, (source, target) in enumerate(((qg_in, qg_ref), (kg_in, kg_ref)))
    ]
    for copy in gains + copies:
        copy.start()
    for copy in gains:
        copy.wait()
    width = qg_ref.shape[0]
    lane = lax.broadcasted_iota(jnp.int32, (2, HEAD_DIM), 1) - shard_ref[0] * width
    row = lax.broadcasted_iota(jnp.int32, (2, HEAD_DIM), 0)
    both = jnp.zeros((2, HEAD_DIM), jnp.float32)
    for i in range(width):
        both = jnp.where(lane == i, jnp.where(row == 0, qg_ref[i], kg_ref[i]), both)
    gain_ref[...] = jnp.broadcast_to(both[None], gain_ref.shape)
    for copy in copies:
        copy.wait()


def pack(k, v, q_gain, k_gain, shard, shards):
    return pl.pallas_call(
        pack_kernel,
        in_specs=[HBM_IN] * 4 + [SMEM_IN],
        out_specs=[VMEM_IN, VMEM_IN],
        out_shape=[
            pltpu.VMEM((ROWS, 2 * KV_HEADS * HEAD_DIM), jnp.bfloat16),
            pltpu.VMEM((shards, 2, HEAD_DIM), jnp.float32),
        ],
        scratch_shapes=[
            pltpu.SMEM(q_gain.shape, jnp.float32),
            pltpu.SMEM(k_gain.shape, jnp.float32),
            pltpu.SemaphoreType.DMA((2 * KV_HEADS + 2,)),
        ],
        compiler_params=pltpu.CompilerParams(vmem_limit_bytes=VMEM),
        name="pack",
    )(*in_hbm(k, v, q_gain, k_gain), shard)


def forward_keys(raw, gain, cosine, sine):
    x = raw.astype(jnp.float32)
    unit = x * lax.rsqrt(jnp.mean(x * x, axis=-1, keepdims=True) + norm_epsilon)
    straight, across = unit * cosine, roll_half(unit) * sine
    return straight, across, (straight * gain + across * roll_half(gain)).astype(jnp.bfloat16)


def over(a, b):
    return jnp.concatenate([a, b], axis=0)


def beside(a, b):
    return jnp.concatenate([a, b], axis=1)


def wide(a):
    return jnp.concatenate([a] * GROUP, axis=1)


def tall(a):
    return jnp.concatenate([a] * GROUP, axis=0)


def attend_kernel(
    q_first, do_first, q_in, do_in, own_ref, one_ref, two_ref, table_ref, row_ref, gain_ref,
    dq_out, ret1_out, ret2_out, keep_ref, gains_ref, q_rest, do_rest, dq_ref, ret1_ref, ret2_ref, q_total, k_total, in_sems, sems,
):
    group, pair = GROUP * HEAD_DIM, 2 * HEAD_DIM

    ahead = q_first.shape[1]
    fetch = [
        pltpu.make_async_copy(source.at[:, pl.ds(ahead, target.shape[1])], target, in_sems.at[n])
        for n, (source, target) in enumerate(((q_in, q_rest), (do_in, do_rest)))
    ]
    for copy in fetch:
        copy.start()

    gain = jnp.sum(gain_ref[...], axis=0)
    kg = gain[1:2]
    qgt = jnp.broadcast_to(gain[0:1], (HEAD_DIM, HEAD_DIM)).T
    cos0, sin0 = table_ref[0], table_ref[1]
    cost, sint = cos0.T, sin0.T
    turn, cross, uncross = wide(qgt * cost), wide(swap_halves(qgt) * sint), wide(qgt * sint)

    row = lax.broadcasted_iota(jnp.int32, (ROWS, ROWS), 0).astype(jnp.float32)
    lane = lax.broadcasted_iota(jnp.int32, (ROWS, ROWS), 1).astype(jnp.float32)
    first = jnp.concatenate([row_ref[0]] * (ROWS // 8), axis=0)
    late_f = jnp.where(first < -ROWS, 1.0, 0.0)
    latet = wide(late_f.astype(jnp.bfloat16))
    on_timet = wide((1.0 - late_f).astype(jnp.bfloat16))
    late_f = late_f.T
    late = tall(late_f.astype(jnp.bfloat16))
    on_time = tall((1.0 - late_f).astype(jnp.bfloat16))
    take = row >= jnp.broadcast_to(first[:, 0:1], row.shape) + 2 * ROWS
    own = (row <= lane) & (row >= first)
    bias = over(
        wide(jnp.where(row >= first + ROWS, 0.0, MASKED)),
        wide(jnp.where(own | (row >= first + 2 * ROWS), 0.0, MASKED)),
    )

    def back(n):
        cosine, sine = row_ref[2 * n - 1][0:1], row_ref[2 * n][0:1]
        return cos0 * cosine + sin0 * sine, sin0 * cosine - cos0 * sine

    cos1, sin1 = back(1)
    cos2, sin2 = back(2)
    cos2, sin2 = jnp.where(take, cos2, cos0), jnp.where(take, sin2, sin0)
    q_total[...] = jnp.zeros_like(q_total)
    k_total[...] = jnp.zeros_like(k_total)

    def out(step):
        copies = []
        for n, (source, target) in enumerate(((dq_ref, dq_out), (ret1_ref, ret1_out), (ret2_ref, ret2_out))):
            width = OUT_HEADS * (group if n == 0 else pair)
            at = pl.ds(step * width, width)
            copies.append(pltpu.make_async_copy(source.at[:, at], target.at[:, at], sems.at[n, step]))
        return copies

    def one_head(head):
        heads = slice(head * group, (head + 1) * group)
        at_k = slice(head * pair, head * pair + HEAD_DIM)
        at_v = slice(head * pair + HEAD_DIM, (head + 1) * pair)
        among = heads
        q_ref, do_ref = q_first, do_first
        if head >= FIRST_HEADS:
            among = slice(head * group - ahead, (head + 1) * group - ahead)
            q_ref, do_ref = q_rest, do_rest
        xt = beside_heads(q_ref[:, among].T).astype(jnp.float32)
        inv_q = lax.rsqrt(jnp.mean(xt * xt, axis=0, keepdims=True) + norm_epsilon)
        qt = ((xt * turn + swap_halves(xt) * cross) * inv_q).astype(jnp.bfloat16)
        q = jnp.concatenate([qt[:, h * ROWS:(h + 1) * ROWS].T for h in range(GROUP)], axis=0)
        do = stack_heads(do_ref[:, among])
        dot_ = beside_heads(do_ref[:, among].T)
        qt_wide = over(qt * on_timet, qt * latet)
        dot_wide = over(dot_ * on_timet, dot_ * latet)
        q_wide = beside(q * on_time, q * late)
        do_wide = beside(do * on_time, do * late)

        v0, v1 = own_ref[:, at_v], one_ref[:, at_v]
        v2 = jnp.where(take, two_ref[:, at_v], v0)
        straight0, across0, k0 = forward_keys(own_ref[:, at_k], kg, cos0, sin0)
        straight1, across1, k1 = forward_keys(one_ref[:, at_k], kg, cos1, sin1)
        straight2, across2, k2 = forward_keys(jnp.where(take, two_ref[:, at_k], own_ref[:, at_k]), kg, cos2, sin2)
        k_all = over(beside(k1, k1), beside(k0, k2))
        v_all = over(beside(v1, v1), beside(v0, v2))
        k1t = k1.T
        kt_all = over(beside(k1t, k0.T), beside(k1t, k2.T))

        s = dot(k_all, qt_wide, NN) * (HEAD_DIM ** (-0.5) * LOG2E) + bias
        w = jnp.exp2(s - jnp.max(s, axis=0, keepdims=True))
        p = w * (1.0 / jnp.sum(w, axis=0, keepdims=True))
        dp = dot(v_all, dot_wide, NN)
        delta = jnp.sum(p * dp, axis=0, keepdims=True)
        ds = (p * (dp - delta) * (HEAD_DIM ** (-0.5))).astype(jnp.bfloat16)

        dv = dot(p.astype(jnp.bfloat16), do_wide, NN)
        dk = dot(ds, q_wide, NN)
        dk1, dv1 = dk[:ROWS, :HEAD_DIM] + dk[:ROWS, HEAD_DIM:], dv[:ROWS, :HEAD_DIM] + dv[:ROWS, HEAD_DIM:]
        dk0, dk2 = dk[ROWS:, :HEAD_DIM], dk[ROWS:, HEAD_DIM:]
        dv0, dv2 = dv[ROWS:, :HEAD_DIM], dv[ROWS:, HEAD_DIM:]

        dqt = dot(kt_all, ds, NN)
        dqt = jnp.where(latet > 0.0, dqt[HEAD_DIM:], dqt[:HEAD_DIM])
        dqt = dqt.astype(jnp.bfloat16).astype(jnp.float32)
        et = dqt * turn - swap_halves(dqt) * uncross
        ext = et * xt
        mean = jnp.mean(ext, axis=0, keepdims=True)
        dxt = (et * inv_q - xt * (inv_q * inv_q * inv_q * mean)).astype(jnp.bfloat16)
        dq_ref[:, heads] = over_heads(dxt).T
        ext = ext * inv_q
        q_total[...] += sum(ext[:, h * ROWS:(h + 1) * ROWS] for h in range(GROUP))
        k_total[0] += fold8(dk0 * straight0 + dk1 * straight1 + dk2 * straight2)
        k_total[1] += fold8(dk0 * across0 + dk1 * across1 + dk2 * across2)

        ret1_ref[:, at_k] = dk1.astype(jnp.bfloat16)
        ret1_ref[:, at_v] = dv1.astype(jnp.bfloat16)
        ret2_ref[:, at_k] = jnp.where(take, dk2, 0.0).astype(jnp.bfloat16)
        ret2_ref[:, at_v] = jnp.where(take, dv2, 0.0).astype(jnp.bfloat16)
        keep_ref[:, at_k] = dk0 + jnp.where(take, 0.0, dk2)
        keep_ref[:, at_v] = dv0 + jnp.where(take, 0.0, dv2)

    for head in range(KV_HEADS):
        if head == FIRST_HEADS:
            for copy in fetch:
                copy.wait()
        one_head(head)
        if head % OUT_HEADS == OUT_HEADS - 1:
            for copy in out(head // OUT_HEADS):
                copy.start()

    q_gain_grad = jnp.sum(q_total[...].T, axis=0, keepdims=True) / gain[0:1]
    k_gain_grad = jnp.sum(k_total[0] + roll_half(k_total[1]), axis=0, keepdims=True)
    gains_ref[...] = jnp.broadcast_to(over(q_gain_grad, k_gain_grad)[None], gains_ref.shape)

    for step in range(KV_HEADS // OUT_HEADS):
        for copy in out(step):
            copy.wait()


def attend(q_first, do_first, q, do, own, one, two, tables, peers):
    pair = (ROWS, 2 * KV_HEADS * HEAD_DIM)
    return pl.pallas_call(
        attend_kernel,
        in_specs=[VMEM_IN] * 2 + [HBM_IN] * 2 + [VMEM_IN] * 6,
        out_specs=[HBM_IN] * 3 + [VMEM_IN] * 2,
        out_shape=[
            pltpu.HBM(q.shape, jnp.bfloat16),
            pltpu.HBM(pair, jnp.bfloat16),
            pltpu.HBM(pair, jnp.bfloat16),
            pltpu.VMEM(pair, jnp.float32),
            pltpu.VMEM((peers, 2, HEAD_DIM), jnp.float32),
        ],
        scratch_shapes=[
            pltpu.VMEM((ROWS, q.shape[1] - q_first.shape[1]), jnp.bfloat16),
            pltpu.VMEM((ROWS, q.shape[1] - q_first.shape[1]), jnp.bfloat16),
            pltpu.VMEM(q.shape, jnp.bfloat16),
            pltpu.VMEM(pair, jnp.bfloat16),
            pltpu.VMEM(pair, jnp.bfloat16),
            pltpu.VMEM((HEAD_DIM, HEAD_DIM), jnp.float32),
            pltpu.VMEM((2, 8, HEAD_DIM), jnp.float32),
            pltpu.SemaphoreType.DMA((2,)),
            pltpu.SemaphoreType.DMA((3, KV_HEADS // OUT_HEADS)),
        ],
        compiler_params=pltpu.CompilerParams(vmem_limit_bytes=VMEM),
        name="attend",
    )(q_first, do_first, *in_hbm(q, do), own, one, two, *tables)


def add_up_kernel(parts_ref, out_ref):
    total = jnp.sum(parts_ref[...], axis=0, keepdims=True)
    out_ref[...] = jnp.broadcast_to(total, out_ref.shape)


def add_up(parts, peers):
    return pl.pallas_call(
        add_up_kernel,
        in_specs=[VMEM_IN],
        out_specs=VMEM_IN,
        out_shape=jax.ShapeDtypeStruct((peers,) + parts.shape[1:], parts.dtype),
        compiler_params=pltpu.CompilerParams(vmem_limit_bytes=VMEM),
        name="add_up",
    )(parts)


def finish_kernel(own_ref, keep_ref, one_ref, two_ref, table_ref, gain_ref, dk_ref, dv_ref, stage, sems):
    gain = jnp.sum(gain_ref[...], axis=0)[1:2]
    copies = []
    for h in range(KV_HEADS):
        at_k, at_v = pl.ds(2 * h * HEAD_DIM, HEAD_DIM), pl.ds((2 * h + 1) * HEAD_DIM, HEAD_DIM)
        dk, dv = (keep_ref[:, at] + one_ref[:, at] + two_ref[:, at] for at in (at_k, at_v))
        x = own_ref[:, at_k].astype(jnp.float32)
        inverse = lax.rsqrt(jnp.mean(x * x, axis=-1, keepdims=True) + norm_epsilon)
        dk = dk.astype(jnp.bfloat16).astype(jnp.float32)
        e = unrotate(dk, table_ref[0], table_ref[1]) * gain
        mean = jnp.mean(e * x, axis=-1, keepdims=True)
        stage[0, h] = (inverse * (e - x * (inverse * inverse * mean))).astype(jnp.bfloat16)
        stage[1, h] = dv.astype(jnp.bfloat16)
        for n, ref in enumerate((dk_ref, dv_ref)):
            at = pl.ds(h * HEAD_DIM, HEAD_DIM)
            copies.append(pltpu.make_async_copy(stage.at[n, h], ref.at[:, at], sems.at[n, h]))
            copies[-1].start()
    for copy in copies:
        copy.wait()


def finish(own, keep, one, two, table, gain):
    out = jax.ShapeDtypeStruct((ROWS, KV_HEADS * HEAD_DIM), jnp.bfloat16)
    return pl.pallas_call(
        finish_kernel,
        in_specs=[VMEM_IN] * 6,
        out_specs=[HBM_IN] * 2,
        out_shape=[out, out],
        scratch_shapes=[
            pltpu.VMEM((2, KV_HEADS, ROWS, HEAD_DIM), jnp.bfloat16),
            pltpu.SemaphoreType.DMA((2, KV_HEADS)),
        ],
        compiler_params=pltpu.CompilerParams(vmem_limit_bytes=VMEM),
        name="finish",
    )(own, keep, one, two, table, gain)


AXES = ("seq", "fsdp")


def device_at(y, z, x, core):
    return ((y % 4 * 4 + x) * 2 + core) * 16 + y // 4 * 8 + z


def gain_groups():
    return [
        [device_at(a, z, x, c) for z in range(8)] + [device_at(4 + (a + 2) % 4, z, x, c) for z in range(8)]
        for a in range(4) for x in range(4) for c in range(2)
    ]


def plane_groups():
    return [[device_at(y, z, x, c) for z in range(8) for x in range(4) for c in range(2)] for y in range(8)]


def column_groups():
    return [[device_at(y, z, x, c) for y in range(8)] for z in range(8) for x in range(4) for c in range(2)]


def swap(rows, groups):
    return lax.all_to_all(rows, AXES, 0, 0, axis_index_groups=groups, tiled=True)


def local(query_raw, key_raw, value_proj, out_grad, query_gain, key_gain, turn_lengths):
    me, shard = lax.axis_index("seq"), lax.axis_index("fsdp")
    seq, shards = lax.axis_size("seq"), lax.axis_size("fsdp")
    base = me * ROWS

    own, gain = pack(key_raw[0], value_proj[0], query_gain, key_gain, shard[None], shards)
    table, rows, q_first, do_first = block_tables(turn_lengths[0], base[None], query_raw[0], out_grad[0])
    two = lax.ppermute(own, "seq", [(i, i + 2) for i in range(seq - 2)])
    one = lax.ppermute(own, "seq", [(i, i + 1) for i in range(seq - 1)])
    gain = swap(gain, gain_groups())
    q_grad, ret1, ret2, keep, parts = attend(q_first, do_first, query_raw[0], out_grad[0], own, one, two, (table, rows, gain), 64)

    back2 = lax.ppermute(ret2, "seq", [(i + 2, i) for i in range(seq - 2)])
    part = add_up(swap(parts, plane_groups()), 8)
    ret1, part = lax.optimization_barrier((ret1, part))
    back1 = lax.ppermute(ret1, "seq", [(i + 1, i) for i in range(seq - 1)])
    total = swap(part, column_groups())
    k_grad, v_grad = finish(own, keep, back1, back2, table, gain)
    total, k_grad, v_grad = lax.optimization_barrier((total, k_grad, v_grad))
    total = jnp.sum(total, axis=0)
    shard_rows = total.reshape(2, shards, HEAD_DIM // shards)
    gain_grad = lax.dynamic_slice_in_dim(shard_rows, shard, 1, axis=1)

    return q_grad[None], k_grad[None], v_grad[None], gain_grad[0, 0], gain_grad[1, 0]


def solution(mesh):
    return jax.shard_map(
        local,
        mesh=mesh,
        in_specs=(
            P("fsdp", "seq", None),
            P("fsdp", "seq", None),
            P("fsdp", "seq", None),
            P("fsdp", "seq", None),
            P("fsdp"),
            P("fsdp"),
            P("fsdp", None),
        ),
        out_specs=(
            P("fsdp", "seq", None),
            P("fsdp", "seq", None),
            P("fsdp", "seq", None),
            P("fsdp"),
            P("fsdp"),
        ),
        check_vma=False,
    )
```

```python
import jax
import jax.numpy as jnp
import numpy as np
from jax import lax
from jax.experimental import pallas as pl
from jax.experimental.pallas import tpu as pltpu
from jax.sharding import PartitionSpec as P

HEADS = 32
KV_HEADS = 8
GROUP = HEADS // KV_HEADS
HEAD_DIM = 128
HALF = HEAD_DIM // 2
ROWS = 128

norm_epsilon = 1e-06
rope_base = 1000000.0
MASKED = -1e30
LOG2E = 1.4426950408889634
OUT_HEADS = 2
FIRST_HEADS = 2
VMEM = 24 * 1024 * 1024
FILL = 3

NT = (((1,), (1,)), ((), ()))
NN = (((1,), (0,)), ((), ()))
TN = (((0,), (0,)), ((), ()))


def dot(a, b, dims):
    return lax.dot_general(a, b, dims, preferred_element_type=jnp.float32)


def roll_half(x):
    return pltpu.roll(x, HALF, axis=1)


def forward_norm(raw, gain, cosine, sine):
    x = raw.astype(jnp.float32)
    inverse = lax.rsqrt(jnp.mean(x * x, axis=-1, keepdims=True) + norm_epsilon)
    y = x * inverse * gain
    return x, inverse, (y * cosine + roll_half(y) * sine).astype(jnp.bfloat16)


def unrotate(grad, cosine, sine):
    return grad * cosine - roll_half(grad) * sine


def swap_halves(x):
    return jnp.concatenate([x[HALF:], x[:HALF]], axis=0)


def beside_heads(x):
    return jnp.concatenate([x[h * HEAD_DIM:(h + 1) * HEAD_DIM] for h in range(GROUP)], axis=1)


def over_heads(x):
    return jnp.concatenate([x[:, h * ROWS:(h + 1) * ROWS] for h in range(GROUP)], axis=0)


def fold8(x):
    return jnp.sum(x.reshape(x.shape[0] // 8, 8, x.shape[1]), axis=0)


def stack_heads(x):
    return jnp.concatenate([x[:, h * HEAD_DIM:(h + 1) * HEAD_DIM] for h in range(GROUP)], axis=0)


def table_kernel(len_ref, place_ref, freq_ref, q_in, do_in, table_ref, row_ref, q_ref, do_ref, sems):
    copies = [
        pltpu.make_async_copy(source.at[:, pl.ds(0, target.shape[1])], target, sems.at[n])
        for n, (source, target) in enumerate(((q_in, q_ref), (do_in, do_ref)))
    ]
    for copy in copies:
        copy.start()
    base = place_ref[0]
    freqs = freq_ref[...]
    token = lax.broadcasted_iota(jnp.int32, (ROWS, HEAD_DIM), 0) + base
    angles = token.astype(jnp.float32) * freqs
    table_ref[0] = jnp.cos(angles)
    table_ref[1] = signed(jnp.sin(angles))

    here = lax.broadcasted_iota(jnp.int32, (8, ROWS), 1)
    first = jnp.zeros((8, ROWS), jnp.int32) - base
    end = -base
    for k in range(len_ref.shape[0] - 1):
        end = end + len_ref[k]
        first = jnp.where(here >= end, end, first)
    row_ref[0] = first.astype(jnp.float32)
    for n in (1, 2):
        angle = jnp.broadcast_to(freqs * float(n * ROWS), (8, HEAD_DIM))
        row_ref[2 * n - 1] = jnp.cos(angle)
        row_ref[2 * n] = signed(jnp.sin(angle))
    for copy in copies:
        copy.wait()


def signed(sine):
    lane = lax.broadcasted_iota(jnp.int32, sine.shape, 1)
    return jnp.where(lane < HALF, -sine, sine)


SMEM_IN = pl.BlockSpec(memory_space=pltpu.SMEM)
VMEM_IN = pl.BlockSpec(memory_space=pltpu.VMEM)
HBM_IN = pl.BlockSpec(memory_space=pltpu.HBM)


def in_hbm(*arrays):
    return [pltpu.with_memory_space_constraint(a, pltpu.HBM) for a in arrays]


def block_tables(lengths, place, q, do):
    half = rope_base ** (-np.arange(HALF) * 2.0 / HEAD_DIM)
    freqs = jnp.asarray(np.concatenate([half, half])[None], jnp.float32)
    return pl.pallas_call(
        table_kernel,
        in_specs=[SMEM_IN, SMEM_IN, VMEM_IN, HBM_IN, HBM_IN],
        out_specs=[VMEM_IN] * 4,
        out_shape=[
            pltpu.VMEM((2, ROWS, HEAD_DIM), jnp.float32),
            pltpu.VMEM((5, 8, HEAD_DIM), jnp.float32),
            pltpu.VMEM((ROWS, FIRST_HEADS * GROUP * HEAD_DIM), q.dtype),
            pltpu.VMEM((ROWS, FIRST_HEADS * GROUP * HEAD_DIM), q.dtype),
        ],
        scratch_shapes=[pltpu.SemaphoreType.DMA((2,))],
        compiler_params=pltpu.CompilerParams(vmem_limit_bytes=VMEM),
        name="tables",
    )(lengths, place, freqs, *in_hbm(q, do))


def pack_kernel(k_ref, v_ref, qg_in, kg_in, shard_ref, own_ref, gain_ref, qg_ref, kg_ref, sems):
    copies = [
        pltpu.make_async_copy(
            ref.at[:, pl.ds(h * HEAD_DIM, HEAD_DIM)],
            own_ref.at[:, pl.ds((2 * h + n) * HEAD_DIM, HEAD_DIM)],
            sems.at[2 * h + n],
        )
        for h in range(KV_HEADS) for n, ref in enumerate((k_ref, v_ref))
    ]
    gains = [
        pltpu.make_async_copy(source, target, sems.at[2 * KV_HEADS + n])
        for n, (source, target) in enumerate(((qg_in, qg_ref), (kg_in, kg_ref)))
    ]
    for copy in gains + copies:
        copy.start()
    for copy in gains:
        copy.wait()
    width = qg_ref.shape[0]
    lane = lax.broadcasted_iota(jnp.int32, (2, HEAD_DIM), 1) - shard_ref[0] * width
    row = lax.broadcasted_iota(jnp.int32, (2, HEAD_DIM), 0)
    both = jnp.zeros((2, HEAD_DIM), jnp.float32)
    for i in range(width):
        both = jnp.where(lane == i, jnp.where(row == 0, qg_ref[i], kg_ref[i]), both)
    gain_ref[...] = jnp.broadcast_to(both[None], gain_ref.shape)
    for copy in copies:
        copy.wait()


def pack(k, v, q_gain, k_gain, shard, shards):
    return pl.pallas_call(
        pack_kernel,
        in_specs=[HBM_IN] * 4 + [SMEM_IN],
        out_specs=[VMEM_IN, VMEM_IN],
        out_shape=[
            pltpu.VMEM((ROWS, 2 * KV_HEADS * HEAD_DIM), jnp.bfloat16),
            pltpu.VMEM((shards, 2, HEAD_DIM), jnp.float32),
        ],
        scratch_shapes=[
            pltpu.SMEM(q_gain.shape, jnp.float32),
            pltpu.SMEM(k_gain.shape, jnp.float32),
            pltpu.SemaphoreType.DMA((2 * KV_HEADS + 2,)),
        ],
        compiler_params=pltpu.CompilerParams(vmem_limit_bytes=VMEM),
        name="pack",
    )(*in_hbm(k, v, q_gain, k_gain), shard)


def forward_keys(raw, gain, cosine, sine):
    x = raw.astype(jnp.float32)
    unit = x * lax.rsqrt(jnp.mean(x * x, axis=-1, keepdims=True) + norm_epsilon)
    straight, across = unit * cosine, roll_half(unit) * sine
    return straight, across, (straight * gain + across * roll_half(gain)).astype(jnp.bfloat16)


def over(a, b):
    return jnp.concatenate([a, b], axis=0)


def beside(a, b):
    return jnp.concatenate([a, b], axis=1)


def wide(a):
    return jnp.concatenate([a] * GROUP, axis=1)


def tall(a):
    return jnp.concatenate([a] * GROUP, axis=0)


def attend_kernel(
    q_first, do_first, q_in, do_in, own_ref, one_ref, two_ref, table_ref, row_ref, gain_ref,
    dq_out, ret1_out, ret2_out, keep_ref, gains_out, gains_ref, q_rest, do_rest, dq_ref, ret1_ref, ret2_ref, q_total, k_total, in_sems, sems,
):
    group, pair = GROUP * HEAD_DIM, 2 * HEAD_DIM

    ahead = q_first.shape[1]
    fetch = [
        pltpu.make_async_copy(source.at[:, pl.ds(ahead, target.shape[1])], target, in_sems.at[n])
        for n, (source, target) in enumerate(((q_in, q_rest), (do_in, do_rest)))
    ]
    for copy in fetch:
        copy.start()

    gain = jnp.sum(gain_ref[...], axis=0)
    kg = gain[1:2]
    qgt = jnp.broadcast_to(gain[0:1], (HEAD_DIM, HEAD_DIM)).T
    cos0, sin0 = table_ref[0], table_ref[1]
    cost, sint = cos0.T, sin0.T
    turn, cross, uncross = wide(qgt * cost), wide(swap_halves(qgt) * sint), wide(qgt * sint)

    row = lax.broadcasted_iota(jnp.int32, (ROWS, ROWS), 0).astype(jnp.float32)
    lane = lax.broadcasted_iota(jnp.int32, (ROWS, ROWS), 1).astype(jnp.float32)
    first = jnp.concatenate([row_ref[0]] * (ROWS // 8), axis=0)
    late_f = jnp.where(first < -ROWS, 1.0, 0.0)
    latet = wide(late_f.astype(jnp.bfloat16))
    on_timet = wide((1.0 - late_f).astype(jnp.bfloat16))
    late_f = late_f.T
    late = tall(late_f.astype(jnp.bfloat16))
    on_time = tall((1.0 - late_f).astype(jnp.bfloat16))
    take = row >= jnp.broadcast_to(first[:, 0:1], row.shape) + 2 * ROWS
    own = (row <= lane) & (row >= first)
    bias = over(
        wide(jnp.where(row >= first + ROWS, 0.0, MASKED)),
        wide(jnp.where(own | (row >= first + 2 * ROWS), 0.0, MASKED)),
    )

    def back(n):
        cosine, sine = row_ref[2 * n - 1][0:1], row_ref[2 * n][0:1]
        return cos0 * cosine + sin0 * sine, sin0 * cosine - cos0 * sine

    cos1, sin1 = back(1)
    cos2, sin2 = back(2)
    cos2, sin2 = jnp.where(take, cos2, cos0), jnp.where(take, sin2, sin0)
    q_total[...] = jnp.zeros_like(q_total)
    k_total[...] = jnp.zeros_like(k_total)

    def out(step):
        copies = []
        for n, (source, target) in enumerate(((dq_ref, dq_out), (ret1_ref, ret1_out), (ret2_ref, ret2_out))):
            width = OUT_HEADS * (group if n == 0 else pair)
            at = pl.ds(step * width, width)
            copies.append(pltpu.make_async_copy(source.at[:, at], target.at[:, at], sems.at[n, step]))
        return copies

    def one_head(head):
        heads = slice(head * group, (head + 1) * group)
        at_k = slice(head * pair, head * pair + HEAD_DIM)
        at_v = slice(head * pair + HEAD_DIM, (head + 1) * pair)
        among = heads
        q_ref, do_ref = q_first, do_first
        if head >= FIRST_HEADS:
            among = slice(head * group - ahead, (head + 1) * group - ahead)
            q_ref, do_ref = q_rest, do_rest
        xt = beside_heads(q_ref[:, among].T).astype(jnp.float32)
        inv_q = lax.rsqrt(jnp.mean(xt * xt, axis=0, keepdims=True) + norm_epsilon)
        qt = ((xt * turn + swap_halves(xt) * cross) * inv_q).astype(jnp.bfloat16)
        q = jnp.concatenate([qt[:, h * ROWS:(h + 1) * ROWS].T for h in range(GROUP)], axis=0)
        do = stack_heads(do_ref[:, among])
        dot_ = beside_heads(do_ref[:, among].T)
        qt_wide = over(qt * on_timet, qt * latet)
        dot_wide = over(dot_ * on_timet, dot_ * latet)
        q_wide = beside(q * on_time, q * late)
        do_wide = beside(do * on_time, do * late)

        v0, v1 = own_ref[:, at_v], one_ref[:, at_v]
        v2 = jnp.where(take, two_ref[:, at_v], v0)
        straight0, across0, k0 = forward_keys(own_ref[:, at_k], kg, cos0, sin0)
        straight1, across1, k1 = forward_keys(one_ref[:, at_k], kg, cos1, sin1)
        straight2, across2, k2 = forward_keys(jnp.where(take, two_ref[:, at_k], own_ref[:, at_k]), kg, cos2, sin2)
        k_all = over(beside(k1, k1), beside(k0, k2))
        v_all = over(beside(v1, v1), beside(v0, v2))
        k1t = k1.T
        kt_all = over(beside(k1t, k0.T), beside(k1t, k2.T))

        s = dot(k_all, qt_wide, NN) * (HEAD_DIM ** (-0.5) * LOG2E) + bias
        w = jnp.exp2(s - jnp.max(s, axis=0, keepdims=True))
        p = w * (1.0 / jnp.sum(w, axis=0, keepdims=True))
        dp = dot(v_all, dot_wide, NN)
        delta = jnp.sum(p * dp, axis=0, keepdims=True)
        ds = (p * (dp - delta) * (HEAD_DIM ** (-0.5))).astype(jnp.bfloat16)

        dv = dot(p.astype(jnp.bfloat16), do_wide, NN)
        dk = dot(ds, q_wide, NN)
        dk1, dv1 = dk[:ROWS, :HEAD_DIM] + dk[:ROWS, HEAD_DIM:], dv[:ROWS, :HEAD_DIM] + dv[:ROWS, HEAD_DIM:]
        dk0, dk2 = dk[ROWS:, :HEAD_DIM], dk[ROWS:, HEAD_DIM:]
        dv0, dv2 = dv[ROWS:, :HEAD_DIM], dv[ROWS:, HEAD_DIM:]

        dqt = dot(kt_all, ds, NN)
        dqt = jnp.where(latet > 0.0, dqt[HEAD_DIM:], dqt[:HEAD_DIM])
        dqt = dqt.astype(jnp.bfloat16).astype(jnp.float32)
        et = dqt * turn - swap_halves(dqt) * uncross
        ext = et * xt
        mean = jnp.mean(ext, axis=0, keepdims=True)
        dxt = (et * inv_q - xt * (inv_q * inv_q * inv_q * mean)).astype(jnp.bfloat16)
        dq_ref[:, heads] = over_heads(dxt).T
        ext = ext * inv_q
        q_total[...] += sum(ext[:, h * ROWS:(h + 1) * ROWS] for h in range(GROUP))
        k_total[0] += fold8(dk0 * straight0 + dk1 * straight1 + dk2 * straight2)
        k_total[1] += fold8(dk0 * across0 + dk1 * across1 + dk2 * across2)

        ret1_ref[:, at_k] = dk1.astype(jnp.bfloat16)
        ret1_ref[:, at_v] = dv1.astype(jnp.bfloat16)
        ret2_ref[:, at_k] = jnp.where(take, dk2, 0.0).astype(jnp.bfloat16)
        ret2_ref[:, at_v] = jnp.where(take, dv2, 0.0).astype(jnp.bfloat16)
        keep_ref[:, at_k] = dk0 + jnp.where(take, 0.0, dk2)
        keep_ref[:, at_v] = dv0 + jnp.where(take, 0.0, dv2)

    for head in range(KV_HEADS):
        if head == FIRST_HEADS:
            for copy in fetch:
                copy.wait()
        one_head(head)
        if head % OUT_HEADS == OUT_HEADS - 1:
            for copy in out(head // OUT_HEADS):
                copy.start()

    q_gain_grad = jnp.sum(q_total[...].T, axis=0, keepdims=True) / gain[0:1]
    k_gain_grad = jnp.sum(k_total[0] + roll_half(k_total[1]), axis=0, keepdims=True)
    gains_ref[...] = jnp.broadcast_to(over(q_gain_grad, k_gain_grad)[None], gains_ref.shape)
    gains = pltpu.make_async_copy(gains_ref, gains_out, in_sems.at[2])
    gains.start()

    for step in range(KV_HEADS // OUT_HEADS):
        for copy in out(step):
            copy.wait()
    gains.wait()


def attend(q_first, do_first, q, do, own, one, two, tables, peers):
    pair = (ROWS, 2 * KV_HEADS * HEAD_DIM)
    return pl.pallas_call(
        attend_kernel,
        in_specs=[VMEM_IN] * 2 + [HBM_IN] * 2 + [VMEM_IN] * 6,
        out_specs=[HBM_IN] * 3 + [VMEM_IN, HBM_IN],
        out_shape=[
            pltpu.HBM(q.shape, jnp.bfloat16),
            pltpu.HBM(pair, jnp.bfloat16),
            pltpu.HBM(pair, jnp.bfloat16),
            pltpu.VMEM(pair, jnp.float32),
            pltpu.HBM((peers, 2, HEAD_DIM), jnp.float32),
        ],
        scratch_shapes=[
            pltpu.VMEM((peers, 2, HEAD_DIM), jnp.float32),
            pltpu.VMEM((ROWS, q.shape[1] - q_first.shape[1]), jnp.bfloat16),
            pltpu.VMEM((ROWS, q.shape[1] - q_first.shape[1]), jnp.bfloat16),
            pltpu.VMEM(q.shape, jnp.bfloat16),
            pltpu.VMEM(pair, jnp.bfloat16),
            pltpu.VMEM(pair, jnp.bfloat16),
            pltpu.VMEM((HEAD_DIM, HEAD_DIM), jnp.float32),
            pltpu.VMEM((2, 8, HEAD_DIM), jnp.float32),
            pltpu.SemaphoreType.DMA((3,)),
            pltpu.SemaphoreType.DMA((3, KV_HEADS // OUT_HEADS)),
        ],
        compiler_params=pltpu.CompilerParams(vmem_limit_bytes=VMEM),
        name="attend",
    )(q_first, do_first, *in_hbm(q, do), own, one, two, *tables)


def hint(work):
    return pl.CostEstimate(flops=work * 20_000_000_000, bytes_accessed=work * 40_000_000, transcendentals=0)


def add_up_kernel(parts_ref, out_ref):
    total = jnp.sum(parts_ref[...], axis=0, keepdims=True)
    out_ref[...] = jnp.broadcast_to(total, out_ref.shape)


def add_up(parts, peers, ahead):
    return pl.pallas_call(
        add_up_kernel,
        in_specs=[VMEM_IN],
        out_specs=VMEM_IN,
        out_shape=jax.ShapeDtypeStruct((peers,) + parts.shape[1:], parts.dtype),
        compiler_params=pltpu.CompilerParams(vmem_limit_bytes=VMEM),
        cost_estimate=hint(ahead),
        name="add_up",
    )(parts)


def parity_kernel(odd_ref, parts_ref, mask_ref):
    mask_ref[...] = jnp.zeros_like(mask_ref) + odd_ref[0].astype(jnp.float32)


def parity(odd, parts):
    return pl.pallas_call(
        parity_kernel,
        in_specs=[SMEM_IN, HBM_IN],
        out_specs=VMEM_IN,
        out_shape=jax.ShapeDtypeStruct((8, HEAD_DIM), jnp.float32),
        compiler_params=pltpu.CompilerParams(vmem_limit_bytes=VMEM),
        cost_estimate=hint(FILL),
        name="parity",
    )(odd.astype(jnp.int32)[None], *in_hbm(parts))


def merge_kernel(odd_ref, near_ref, ret_in, keep_in, far_out, keep_ref, ret_ref, far_ref, in_sems, sems):
    pieces = sems.shape[0]
    width = near_ref.shape[1] // pieces
    odd = jnp.concatenate([odd_ref[0:1]] * (width // HEAD_DIM), axis=1)

    def fetch(n):
        at = pl.ds(n * width, width)
        return pltpu.make_async_copy(ret_in.at[:, at], ret_ref.at[:, at], in_sems.at[n])

    def out(n):
        at = pl.ds(n * width, width)
        return pltpu.make_async_copy(far_ref.at[:, at], far_out.at[:, at], sems.at[n])

    for n in range(pieces):
        fetch(n).start()
    for n in range(pieces):
        at = pl.ds(n * width, width)
        near = near_ref[:, at].astype(jnp.float32)
        fetch(n).wait()
        far_ref[:, at] = (ret_ref[:, at] + near * odd).astype(jnp.bfloat16)
        out(n).start()
        keep_ref[:, at] = keep_in[:, at] + near * (1.0 - odd)
    for n in range(pieces):
        out(n).wait()


def merge(odd, near, ret, keep):
    pieces = 4
    return pl.pallas_call(
        merge_kernel,
        in_specs=[VMEM_IN, VMEM_IN, HBM_IN, VMEM_IN],
        out_specs=[HBM_IN, VMEM_IN],
        out_shape=[pltpu.HBM(ret.shape, ret.dtype), pltpu.VMEM(keep.shape, keep.dtype)],
        input_output_aliases={3: 1},
        scratch_shapes=[
            pltpu.VMEM(ret.shape, ret.dtype),
            pltpu.VMEM(ret.shape, ret.dtype),
            pltpu.SemaphoreType.DMA((pieces,)),
            pltpu.SemaphoreType.DMA((pieces,)),
        ],
        compiler_params=pltpu.CompilerParams(vmem_limit_bytes=VMEM),
        name="merge",
    )(odd, near, *in_hbm(ret), keep)


def finish_kernel(own_ref, keep_ref, far_ref, table_ref, gain_ref, dk_ref, dv_ref, stage, sems):
    gain = jnp.sum(gain_ref[...], axis=0)[1:2]
    copies = []
    for h in range(KV_HEADS):
        at_k, at_v = pl.ds(2 * h * HEAD_DIM, HEAD_DIM), pl.ds((2 * h + 1) * HEAD_DIM, HEAD_DIM)
        dk, dv = (keep_ref[:, at] + far_ref[:, at] for at in (at_k, at_v))
        x = own_ref[:, at_k].astype(jnp.float32)
        inverse = lax.rsqrt(jnp.mean(x * x, axis=-1, keepdims=True) + norm_epsilon)
        dk = dk.astype(jnp.bfloat16).astype(jnp.float32)
        e = unrotate(dk, table_ref[0], table_ref[1]) * gain
        mean = jnp.mean(e * x, axis=-1, keepdims=True)
        stage[0, h] = (inverse * (e - x * (inverse * inverse * mean))).astype(jnp.bfloat16)
        stage[1, h] = dv.astype(jnp.bfloat16)
        for n, ref in enumerate((dk_ref, dv_ref)):
            at = pl.ds(h * HEAD_DIM, HEAD_DIM)
            copies.append(pltpu.make_async_copy(stage.at[n, h], ref.at[:, at], sems.at[n, h]))
            copies[-1].start()
    for copy in copies:
        copy.wait()


def finish(own, keep, far, table, gain):
    out = jax.ShapeDtypeStruct((ROWS, KV_HEADS * HEAD_DIM), jnp.bfloat16)
    return pl.pallas_call(
        finish_kernel,
        in_specs=[VMEM_IN] * 5,
        out_specs=[HBM_IN] * 2,
        out_shape=[out, out],
        scratch_shapes=[
            pltpu.VMEM((2, KV_HEADS, ROWS, HEAD_DIM), jnp.bfloat16),
            pltpu.SemaphoreType.DMA((2, KV_HEADS)),
        ],
        compiler_params=pltpu.CompilerParams(vmem_limit_bytes=VMEM),
        name="finish",
    )(own, keep, far, table, gain)


AXES = ("seq", "fsdp")


def device_at(y, z, x, core):
    return ((y % 4 * 4 + x) * 2 + core) * 16 + y // 4 * 8 + z


def gain_groups():
    return [
        [device_at(a, z, x, c) for z in range(8)] + [device_at(4 + (a + 2) % 4, z, x, c) for z in range(8)]
        for a in range(4) for x in range(4) for c in range(2)
    ]


def plane_groups():
    return [[device_at(y, z, x, c) for z in range(8) for x in range(4) for c in range(2)] for y in range(8)]


def column_groups():
    return [[device_at(y, z, x, c) for y in range(8)] for z in range(8) for x in range(4) for c in range(2)]


def swap(rows, groups):
    return lax.all_to_all(rows, AXES, 0, 0, axis_index_groups=groups, tiled=True)


def local(query_raw, key_raw, value_proj, out_grad, query_gain, key_gain, turn_lengths):
    me, shard = lax.axis_index("seq"), lax.axis_index("fsdp")
    seq, shards = lax.axis_size("seq"), lax.axis_size("fsdp")
    base = me * ROWS
    odd = me % 2 == 1

    own, gain = pack(key_raw[0], value_proj[0], query_gain, key_gain, shard[None], shards)
    table, rows, q_first, do_first = block_tables(turn_lengths[0], base[None], query_raw[0], out_grad[0])
    two = lax.ppermute(own, "seq", [(i, i + 2) for i in range(seq - 2)])
    gain = add_up(swap(gain, gain_groups()), 1, 1)
    one = jnp.where(odd, two, own)
    one, table = lax.optimization_barrier((one, table))
    one = lax.ppermute(one, "seq", [(i, i ^ 1) for i in range(seq)])
    q_grad, ret1, ret2, keep, parts = attend(q_first, do_first, query_raw[0], out_grad[0], own, one, two, (table, rows, gain), 64)

    near = lax.ppermute(ret1, "seq", [(i, i ^ 1) for i in range(seq)])
    far, keep = merge(parity(odd, parts), near, ret2, keep)
    far = lax.ppermute(far, "seq", [(i + 2, i) for i in range(seq - 2)])
    part = add_up(swap(parts, plane_groups()), 8, 1)
    total = swap(part, column_groups())
    k_grad, v_grad = finish(own, keep, far, table, gain)
    total, k_grad, v_grad = lax.optimization_barrier((total, k_grad, v_grad))
    total = jnp.sum(total, axis=0)
    shard_rows = total.reshape(2, shards, HEAD_DIM // shards)
    gain_grad = lax.dynamic_slice_in_dim(shard_rows, shard, 1, axis=1)

    return q_grad[None], k_grad[None], v_grad[None], gain_grad[0, 0], gain_grad[1, 0]


def solution(mesh):
    return jax.shard_map(
        local,
        mesh=mesh,
        in_specs=(
            P("fsdp", "seq", None),
            P("fsdp", "seq", None),
            P("fsdp", "seq", None),
            P("fsdp", "seq", None),
            P("fsdp"),
            P("fsdp"),
            P("fsdp", None),
        ),
        out_specs=(
            P("fsdp", "seq", None),
            P("fsdp", "seq", None),
            P("fsdp", "seq", None),
            P("fsdp"),
            P("fsdp"),
        ),
        check_vma=False,
    )
```

```python
import jax
import jax.numpy as jnp
import numpy as np
from jax import lax
from jax.experimental import pallas as pl
from jax.experimental.pallas import tpu as pltpu
from jax.sharding import PartitionSpec as P

HEADS = 32
KV_HEADS = 8
GROUP = HEADS // KV_HEADS
HEAD_DIM = 128
HALF = HEAD_DIM // 2
ROWS = 128

norm_epsilon = 1e-06
rope_base = 1000000.0
MASKED = -1e30
LOG2E = 1.4426950408889634
OUT_HEADS = 2
FIRST_HEADS = 2
VMEM = 24 * 1024 * 1024

NT = (((1,), (1,)), ((), ()))
NN = (((1,), (0,)), ((), ()))
TN = (((0,), (0,)), ((), ()))


def dot(a, b, dims):
    return lax.dot_general(a, b, dims, preferred_element_type=jnp.float32)


def roll_half(x):
    return pltpu.roll(x, HALF, axis=1)


def unrotate(grad, cosine, sine):
    return grad * cosine - roll_half(grad) * sine


def swap_halves(x):
    return jnp.concatenate([x[HALF:], x[:HALF]], axis=0)


def beside_heads(x):
    return jnp.concatenate([x[h * HEAD_DIM:(h + 1) * HEAD_DIM] for h in range(GROUP)], axis=1)


def over_heads(x):
    return jnp.concatenate([x[:, h * ROWS:(h + 1) * ROWS] for h in range(GROUP)], axis=0)


def fold8(x):
    return jnp.sum(x.reshape(x.shape[0] // 8, 8, x.shape[1]), axis=0)


def stack_heads(x):
    return jnp.concatenate([x[:, h * HEAD_DIM:(h + 1) * HEAD_DIM] for h in range(GROUP)], axis=0)


def table_kernel(len_ref, place_ref, freq_ref, q_in, do_in, table_ref, row_ref, q_ref, do_ref, sems):
    copies = [
        pltpu.make_async_copy(source.at[:, pl.ds(0, target.shape[1])], target, sems.at[n])
        for n, (source, target) in enumerate(((q_in, q_ref), (do_in, do_ref)))
    ]
    for copy in copies:
        copy.start()
    base = place_ref[0]
    freqs = freq_ref[...]
    token = lax.broadcasted_iota(jnp.int32, (ROWS, HEAD_DIM), 0) + base
    angles = token.astype(jnp.float32) * freqs
    table_ref[0] = jnp.cos(angles)
    table_ref[1] = signed(jnp.sin(angles))

    here = lax.broadcasted_iota(jnp.int32, (8, ROWS), 1)
    first = jnp.zeros((8, ROWS), jnp.int32) - base
    end = -base
    for k in range(len_ref.shape[0] - 1):
        end = end + len_ref[k]
        first = jnp.where(here >= end, end, first)
    row_ref[0] = first.astype(jnp.float32)
    for n in (1, 2):
        angle = jnp.broadcast_to(freqs * float(n * ROWS), (8, HEAD_DIM))
        row_ref[2 * n - 1] = jnp.cos(angle)
        row_ref[2 * n] = signed(jnp.sin(angle))
    for copy in copies:
        copy.wait()


def signed(sine):
    lane = lax.broadcasted_iota(jnp.int32, sine.shape, 1)
    return jnp.where(lane < HALF, -sine, sine)


SMEM_IN = pl.BlockSpec(memory_space=pltpu.SMEM)
VMEM_IN = pl.BlockSpec(memory_space=pltpu.VMEM)
HBM_IN = pl.BlockSpec(memory_space=pltpu.HBM)


def in_hbm(*arrays):
    return [pltpu.with_memory_space_constraint(a, pltpu.HBM) for a in arrays]


def block_tables(lengths, place, q, do):
    half = rope_base ** (-np.arange(HALF) * 2.0 / HEAD_DIM)
    freqs = jnp.asarray(np.concatenate([half, half])[None], jnp.float32)
    return pl.pallas_call(
        table_kernel,
        in_specs=[SMEM_IN, SMEM_IN, VMEM_IN, HBM_IN, HBM_IN],
        out_specs=[VMEM_IN] * 4,
        out_shape=[
            pltpu.VMEM((2, ROWS, HEAD_DIM), jnp.float32),
            pltpu.VMEM((5, 8, HEAD_DIM), jnp.float32),
            pltpu.VMEM((ROWS, FIRST_HEADS * GROUP * HEAD_DIM), q.dtype),
            pltpu.VMEM((ROWS, FIRST_HEADS * GROUP * HEAD_DIM), q.dtype),
        ],
        scratch_shapes=[pltpu.SemaphoreType.DMA((2,))],
        compiler_params=pltpu.CompilerParams(vmem_limit_bytes=VMEM),
        name="tables",
    )(lengths, place, freqs, *in_hbm(q, do))


def pack_kernel(k_ref, v_ref, qg_in, kg_in, shard_ref, own_ref, gain_out, gain_ref, qg_ref, kg_ref, sems):
    copies = [
        pltpu.make_async_copy(
            ref.at[:, pl.ds(h * HEAD_DIM, HEAD_DIM)],
            own_ref.at[:, pl.ds((2 * h + n) * HEAD_DIM, HEAD_DIM)],
            sems.at[2 * h + n],
        )
        for h in range(KV_HEADS) for n, ref in enumerate((k_ref, v_ref))
    ]
    gains = [
        pltpu.make_async_copy(source, target, sems.at[2 * KV_HEADS + n])
        for n, (source, target) in enumerate(((qg_in, qg_ref), (kg_in, kg_ref)))
    ]
    for copy in gains + copies:
        copy.start()
    for copy in gains:
        copy.wait()
    width = qg_ref.shape[0]
    lane = lax.broadcasted_iota(jnp.int32, (2, HEAD_DIM), 1) - shard_ref[0] * width
    row = lax.broadcasted_iota(jnp.int32, (2, HEAD_DIM), 0)
    both = jnp.zeros((2, HEAD_DIM), jnp.float32)
    for i in range(width):
        both = jnp.where(lane == i, jnp.where(row == 0, qg_ref[i], kg_ref[i]), both)
    gain_ref[...] = jnp.broadcast_to(both[None], gain_ref.shape)
    copies.append(pltpu.make_async_copy(gain_ref, gain_out, sems.at[2 * KV_HEADS + 2]))
    copies[-1].start()
    for copy in copies:
        copy.wait()


def pack(k, v, q_gain, k_gain, shard, shards):
    return pl.pallas_call(
        pack_kernel,
        in_specs=[HBM_IN] * 4 + [SMEM_IN],
        out_specs=[VMEM_IN, HBM_IN],
        out_shape=[
            pltpu.VMEM((ROWS, 2 * KV_HEADS * HEAD_DIM), jnp.bfloat16),
            pltpu.HBM((shards, 2, HEAD_DIM), jnp.float32),
        ],
        scratch_shapes=[
            pltpu.VMEM((shards, 2, HEAD_DIM), jnp.float32),
            pltpu.SMEM(q_gain.shape, jnp.float32),
            pltpu.SMEM(k_gain.shape, jnp.float32),
            pltpu.SemaphoreType.DMA((2 * KV_HEADS + 3,)),
        ],
        compiler_params=pltpu.CompilerParams(vmem_limit_bytes=VMEM),
        name="pack",
    )(*in_hbm(k, v, q_gain, k_gain), shard)


def forward_keys(raw, gain, cosine, sine):
    x = raw.astype(jnp.float32)
    unit = x * lax.rsqrt(jnp.mean(x * x, axis=-1, keepdims=True) + norm_epsilon)
    straight, across = unit * cosine, roll_half(unit) * sine
    return straight, across, (straight * gain + across * roll_half(gain)).astype(jnp.bfloat16)


def over(a, b):
    return jnp.concatenate([a, b], axis=0)


def beside(a, b):
    return jnp.concatenate([a, b], axis=1)


def wide(a):
    return jnp.concatenate([a] * GROUP, axis=1)


def tall(a):
    return jnp.concatenate([a] * GROUP, axis=0)


def attend_kernel(
    q_first, do_first, q_in, do_in, own_ref, one_ref, two_ref, table_ref, row_ref, gain_ref,
    dq_out, ret1_out, ret2_out, keep_ref, gains_out, gains_ref, q_rest, do_rest, dq_ref, ret1_ref, ret2_ref, q_total, k_total, in_sems, sems,
):
    group, pair = GROUP * HEAD_DIM, 2 * HEAD_DIM

    ahead = q_first.shape[1]
    fetch = [
        pltpu.make_async_copy(source.at[:, pl.ds(ahead, target.shape[1])], target, in_sems.at[n])
        for n, (source, target) in enumerate(((q_in, q_rest), (do_in, do_rest)))
    ]
    for copy in fetch:
        copy.start()

    gain = jnp.sum(gain_ref[...], axis=0)
    kg = gain[1:2]
    qgt = jnp.broadcast_to(gain[0:1], (HEAD_DIM, HEAD_DIM)).T
    cos0, sin0 = table_ref[0], table_ref[1]
    cost, sint = cos0.T, sin0.T
    turn, cross, uncross = wide(qgt * cost), wide(swap_halves(qgt) * sint), wide(qgt * sint)

    row = lax.broadcasted_iota(jnp.int32, (ROWS, ROWS), 0).astype(jnp.float32)
    lane = lax.broadcasted_iota(jnp.int32, (ROWS, ROWS), 1).astype(jnp.float32)
    first = jnp.concatenate([row_ref[0]] * (ROWS // 8), axis=0)
    late_f = jnp.where(first < -ROWS, 1.0, 0.0)
    latet = wide(late_f.astype(jnp.bfloat16))
    on_timet = wide((1.0 - late_f).astype(jnp.bfloat16))
    late_f = late_f.T
    late = tall(late_f.astype(jnp.bfloat16))
    on_time = tall((1.0 - late_f).astype(jnp.bfloat16))
    take = row >= jnp.broadcast_to(first[:, 0:1], row.shape) + 2 * ROWS
    own = (row <= lane) & (row >= first)
    bias = over(
        wide(jnp.where(row >= first + ROWS, 0.0, MASKED)),
        wide(jnp.where(own | (row >= first + 2 * ROWS), 0.0, MASKED)),
    )

    def back(n):
        cosine, sine = row_ref[2 * n - 1][0:1], row_ref[2 * n][0:1]
        return cos0 * cosine + sin0 * sine, sin0 * cosine - cos0 * sine

    cos1, sin1 = back(1)
    cos2, sin2 = back(2)
    cos2, sin2 = jnp.where(take, cos2, cos0), jnp.where(take, sin2, sin0)
    q_total[...] = jnp.zeros_like(q_total)
    k_total[...] = jnp.zeros_like(k_total)

    def out(step):
        copies = []
        for n, (source, target) in enumerate(((dq_ref, dq_out), (ret1_ref, ret1_out), (ret2_ref, ret2_out))):
            width = OUT_HEADS * (group if n == 0 else pair)
            at = pl.ds(step * width, width)
            copies.append(pltpu.make_async_copy(source.at[:, at], target.at[:, at], sems.at[n, step]))
        return copies

    def one_head(head):
        heads = slice(head * group, (head + 1) * group)
        at_k = slice(head * pair, head * pair + HEAD_DIM)
        at_v = slice(head * pair + HEAD_DIM, (head + 1) * pair)
        among = heads
        q_ref, do_ref = q_first, do_first
        if head >= FIRST_HEADS:
            among = slice(head * group - ahead, (head + 1) * group - ahead)
            q_ref, do_ref = q_rest, do_rest
        xt = beside_heads(q_ref[:, among].T).astype(jnp.float32)
        inv_q = lax.rsqrt(jnp.mean(xt * xt, axis=0, keepdims=True) + norm_epsilon)
        qt = ((xt * turn + swap_halves(xt) * cross) * inv_q).astype(jnp.bfloat16)
        q = jnp.concatenate([qt[:, h * ROWS:(h + 1) * ROWS].T for h in range(GROUP)], axis=0)
        do = stack_heads(do_ref[:, among])
        dot_ = beside_heads(do_ref[:, among].T)
        qt_wide = over(qt * on_timet, qt * latet)
        dot_wide = over(dot_ * on_timet, dot_ * latet)
        q_wide = beside(q * on_time, q * late)
        do_wide = beside(do * on_time, do * late)

        v0, v1 = own_ref[:, at_v], one_ref[:, at_v]
        v2 = jnp.where(take, two_ref[:, at_v], v0)
        straight0, across0, k0 = forward_keys(own_ref[:, at_k], kg, cos0, sin0)
        straight1, across1, k1 = forward_keys(one_ref[:, at_k], kg, cos1, sin1)
        straight2, across2, k2 = forward_keys(jnp.where(take, two_ref[:, at_k], own_ref[:, at_k]), kg, cos2, sin2)
        k_all = over(beside(k1, k1), beside(k0, k2))
        v_all = over(beside(v1, v1), beside(v0, v2))
        k1t = k1.T
        kt_all = over(beside(k1t, k0.T), beside(k1t, k2.T))

        s = dot(k_all, qt_wide, NN) * (HEAD_DIM ** (-0.5) * LOG2E) + bias
        w = jnp.exp2(s - jnp.max(s, axis=0, keepdims=True))
        p = w * (1.0 / jnp.sum(w, axis=0, keepdims=True))
        dp = dot(v_all, dot_wide, NN)
        delta = jnp.sum(p * dp, axis=0, keepdims=True)
        ds = (p * (dp - delta) * (HEAD_DIM ** (-0.5))).astype(jnp.bfloat16)

        dv = dot(p.astype(jnp.bfloat16), do_wide, NN)
        dk = dot(ds, q_wide, NN)
        dk1, dv1 = dk[:ROWS, :HEAD_DIM] + dk[:ROWS, HEAD_DIM:], dv[:ROWS, :HEAD_DIM] + dv[:ROWS, HEAD_DIM:]
        dk0, dk2 = dk[ROWS:, :HEAD_DIM], dk[ROWS:, HEAD_DIM:]
        dv0, dv2 = dv[ROWS:, :HEAD_DIM], dv[ROWS:, HEAD_DIM:]

        dqt = dot(kt_all, ds, NN)
        dqt = jnp.where(latet > 0.0, dqt[HEAD_DIM:], dqt[:HEAD_DIM])
        dqt = dqt.astype(jnp.bfloat16).astype(jnp.float32)
        et = dqt * turn - swap_halves(dqt) * uncross
        ext = et * xt
        mean = jnp.mean(ext, axis=0, keepdims=True)
        dxt = (et * inv_q - xt * (inv_q * inv_q * inv_q * mean)).astype(jnp.bfloat16)
        dq_ref[:, heads] = over_heads(dxt).T
        ext = ext * inv_q
        q_total[...] += sum(ext[:, h * ROWS:(h + 1) * ROWS] for h in range(GROUP))
        k_total[0] += fold8(dk0 * straight0 + dk1 * straight1 + dk2 * straight2)
        k_total[1] += fold8(dk0 * across0 + dk1 * across1 + dk2 * across2)

        ret1_ref[:, at_k] = dk1.astype(jnp.bfloat16)
        ret1_ref[:, at_v] = dv1.astype(jnp.bfloat16)
        ret2_ref[:, at_k] = jnp.where(take, dk2, 0.0).astype(jnp.bfloat16)
        ret2_ref[:, at_v] = jnp.where(take, dv2, 0.0).astype(jnp.bfloat16)
        keep_ref[:, at_k] = dk0 + jnp.where(take, 0.0, dk2)
        keep_ref[:, at_v] = dv0 + jnp.where(take, 0.0, dv2)

    for head in range(KV_HEADS):
        if head == FIRST_HEADS:
            for copy in fetch:
                copy.wait()
        one_head(head)
        if head % OUT_HEADS == OUT_HEADS - 1:
            for copy in out(head // OUT_HEADS):
                copy.start()

    q_gain_grad = jnp.sum(q_total[...].T, axis=0, keepdims=True) / gain[0:1]
    k_gain_grad = jnp.sum(k_total[0] + roll_half(k_total[1]), axis=0, keepdims=True)
    gains_ref[...] = jnp.broadcast_to(over(q_gain_grad, k_gain_grad)[None], gains_ref.shape)
    gains = pltpu.make_async_copy(gains_ref, gains_out, in_sems.at[2])
    gains.start()

    for step in range(KV_HEADS // OUT_HEADS):
        for copy in out(step):
            copy.wait()
    gains.wait()


def attend(q_first, do_first, q, do, own, one, two, tables, peers):
    pair = (ROWS, 2 * KV_HEADS * HEAD_DIM)
    return pl.pallas_call(
        attend_kernel,
        in_specs=[VMEM_IN] * 2 + [HBM_IN] * 2 + [VMEM_IN] * 6,
        out_specs=[HBM_IN] * 3 + [VMEM_IN, HBM_IN],
        out_shape=[
            pltpu.HBM(q.shape, jnp.bfloat16),
            pltpu.HBM(pair, jnp.bfloat16),
            pltpu.HBM(pair, jnp.bfloat16),
            pltpu.VMEM(pair, jnp.float32),
            pltpu.HBM((peers, 2, HEAD_DIM), jnp.float32),
        ],
        scratch_shapes=[
            pltpu.VMEM((peers, 2, HEAD_DIM), jnp.float32),
            pltpu.VMEM((ROWS, q.shape[1] - q_first.shape[1]), jnp.bfloat16),
            pltpu.VMEM((ROWS, q.shape[1] - q_first.shape[1]), jnp.bfloat16),
            pltpu.VMEM(q.shape, jnp.bfloat16),
            pltpu.VMEM(pair, jnp.bfloat16),
            pltpu.VMEM(pair, jnp.bfloat16),
            pltpu.VMEM((HEAD_DIM, HEAD_DIM), jnp.float32),
            pltpu.VMEM((2, 8, HEAD_DIM), jnp.float32),
            pltpu.SemaphoreType.DMA((3,)),
            pltpu.SemaphoreType.DMA((3, KV_HEADS // OUT_HEADS)),
        ],
        compiler_params=pltpu.CompilerParams(vmem_limit_bytes=VMEM),
        name="attend",
    )(q_first, do_first, *in_hbm(q, do), own, one, two, *tables)


def hint(work):
    return pl.CostEstimate(flops=work * 20_000_000_000, bytes_accessed=work * 40_000_000, transcendentals=0)


def add_up_kernel(parts_ref, out_ref):
    total = jnp.sum(parts_ref[...], axis=0, keepdims=True)
    out_ref[...] = jnp.broadcast_to(total, out_ref.shape)


def add_up(parts, peers, ahead):
    return pl.pallas_call(
        add_up_kernel,
        in_specs=[VMEM_IN],
        out_specs=VMEM_IN,
        out_shape=jax.ShapeDtypeStruct((peers,) + parts.shape[1:], parts.dtype),
        compiler_params=pltpu.CompilerParams(vmem_limit_bytes=VMEM),
        cost_estimate=hint(ahead),
        name="add_up",
    )(parts)


def merge_kernel(odd_ref, near_ref, ret_in, keep_in, far_ref, keep_ref, ret_ref, sems):
    pieces = sems.shape[0]
    width = near_ref.shape[1] // pieces
    odd = odd_ref[0].astype(jnp.float32)

    def fetch(n):
        at = pl.ds(n * width, width)
        return pltpu.make_async_copy(ret_in.at[:, at], ret_ref.at[:, at], sems.at[n])

    for n in range(pieces):
        fetch(n).start()
    for n in range(pieces):
        at = pl.ds(n * width, width)
        near = near_ref[:, at].astype(jnp.float32)
        fetch(n).wait()
        far_ref[:, at] = (ret_ref[:, at] + near * odd).astype(jnp.bfloat16)
        keep_ref[:, at] = keep_in[:, at] + near * (1.0 - odd)


def merge(odd, near, ret, keep):
    pieces = 4
    return pl.pallas_call(
        merge_kernel,
        in_specs=[SMEM_IN, VMEM_IN, HBM_IN, VMEM_IN],
        out_specs=[VMEM_IN] * 2,
        out_shape=[pltpu.VMEM(ret.shape, ret.dtype), pltpu.VMEM(keep.shape, keep.dtype)],
        input_output_aliases={3: 1},
        scratch_shapes=[
            pltpu.VMEM(ret.shape, ret.dtype),
            pltpu.SemaphoreType.DMA((pieces,)),
        ],
        compiler_params=pltpu.CompilerParams(vmem_limit_bytes=VMEM),
        name="merge",
    )(odd.astype(jnp.int32)[None], near, *in_hbm(ret), keep)


def finish_kernel(own_ref, keep_ref, far_ref, table_ref, gain_ref, dk_ref, dv_ref, stage, sems):
    gain = jnp.sum(gain_ref[...], axis=0)[1:2]
    copies = []
    for h in range(KV_HEADS):
        at_k, at_v = pl.ds(2 * h * HEAD_DIM, HEAD_DIM), pl.ds((2 * h + 1) * HEAD_DIM, HEAD_DIM)
        dk, dv = (keep_ref[:, at] + far_ref[:, at] for at in (at_k, at_v))
        x = own_ref[:, at_k].astype(jnp.float32)
        inverse = lax.rsqrt(jnp.mean(x * x, axis=-1, keepdims=True) + norm_epsilon)
        dk = dk.astype(jnp.bfloat16).astype(jnp.float32)
        e = unrotate(dk, table_ref[0], table_ref[1]) * gain
        mean = jnp.mean(e * x, axis=-1, keepdims=True)
        stage[0, h] = (inverse * (e - x * (inverse * inverse * mean))).astype(jnp.bfloat16)
        stage[1, h] = dv.astype(jnp.bfloat16)
        for n, ref in enumerate((dk_ref, dv_ref)):
            at = pl.ds(h * HEAD_DIM, HEAD_DIM)
            copies.append(pltpu.make_async_copy(stage.at[n, h], ref.at[:, at], sems.at[n, h]))
            copies[-1].start()
    for copy in copies:
        copy.wait()


def finish(own, keep, far, table, gain):
    out = jax.ShapeDtypeStruct((ROWS, KV_HEADS * HEAD_DIM), jnp.bfloat16)
    return pl.pallas_call(
        finish_kernel,
        in_specs=[VMEM_IN] * 5,
        out_specs=[HBM_IN] * 2,
        out_shape=[out, out],
        scratch_shapes=[
            pltpu.VMEM((2, KV_HEADS, ROWS, HEAD_DIM), jnp.bfloat16),
            pltpu.SemaphoreType.DMA((2, KV_HEADS)),
        ],
        compiler_params=pltpu.CompilerParams(vmem_limit_bytes=VMEM),
        name="finish",
    )(own, keep, far, table, gain)


AXES = ("seq", "fsdp")


def device_at(y, z, x, core):
    return ((y % 4 * 4 + x) * 2 + core) * 16 + y // 4 * 8 + z


def gain_groups():
    return [
        [device_at(a, z, x, c) for z in range(8)] + [device_at(4 + (a + 2) % 4, z, x, c) for z in range(8)]
        for a in range(4) for x in range(4) for c in range(2)
    ]


def plane_groups():
    return [[device_at(y, z, x, c) for z in range(8) for x in range(4) for c in range(2)] for y in range(8)]


def column_groups():
    return [[device_at(y, z, x, c) for y in range(8)] for z in range(8) for x in range(4) for c in range(2)]


def swap(rows, groups):
    return lax.all_to_all(rows, AXES, 0, 0, axis_index_groups=groups, tiled=True)


def local(query_raw, key_raw, value_proj, out_grad, query_gain, key_gain, turn_lengths):
    me, shard = lax.axis_index("seq"), lax.axis_index("fsdp")
    seq, shards = lax.axis_size("seq"), lax.axis_size("fsdp")
    base = me * ROWS
    odd = me % 2 == 1

    own, gain = pack(key_raw[0], value_proj[0], query_gain, key_gain, shard[None], shards)
    table, rows, q_first, do_first = block_tables(turn_lengths[0], base[None], query_raw[0], out_grad[0])
    two = lax.ppermute(own, "seq", [(i, i + 2) for i in range(seq - 2)])
    gain = add_up(swap(gain, gain_groups()), 1, 1)
    one = jnp.where(odd, two, own)
    one, table = lax.optimization_barrier((one, table))
    one = lax.ppermute(one, "seq", [(i, i ^ 1) for i in range(seq)])
    q_grad, ret1, ret2, keep, parts = attend(q_first, do_first, query_raw[0], out_grad[0], own, one, two, (table, rows, gain), 64)

    near = lax.ppermute(ret1, "seq", [(i, i ^ 1) for i in range(seq)])
    far, keep = merge(odd, near, ret2, keep)
    far = lax.ppermute(far, "seq", [(i + 2, i) for i in range(seq - 2)])
    part = add_up(swap(parts, plane_groups()), 8, 1)
    total = swap(part, column_groups())
    k_grad, v_grad = finish(own, keep, far, table, gain)
    total, k_grad, v_grad = lax.optimization_barrier((total, k_grad, v_grad))
    total = jnp.sum(total, axis=0)
    shard_rows = total.reshape(2, shards, HEAD_DIM // shards)
    gain_grad = lax.dynamic_slice_in_dim(shard_rows, shard, 1, axis=1)

    return q_grad[None], k_grad[None], v_grad[None], gain_grad[0, 0], gain_grad[1, 0]


def solution(mesh):
    return jax.shard_map(
        local,
        mesh=mesh,
        in_specs=(
            P("fsdp", "seq", None),
            P("fsdp", "seq", None),
            P("fsdp", "seq", None),
            P("fsdp", "seq", None),
            P("fsdp"),
            P("fsdp"),
            P("fsdp", None),
        ),
        out_specs=(
            P("fsdp", "seq", None),
            P("fsdp", "seq", None),
            P("fsdp", "seq", None),
            P("fsdp"),
            P("fsdp"),
        ),
        check_vma=False,
    )
```

```python
import jax
import jax.numpy as jnp
import numpy as np
from jax import lax
from jax.experimental import pallas as pl
from jax.experimental.pallas import tpu as pltpu
from jax.sharding import PartitionSpec as P

HEADS = 32
KV_HEADS = 8
GROUP = HEADS // KV_HEADS
HEAD_DIM = 128
HALF = HEAD_DIM // 2
ROWS = 128

norm_epsilon = 1e-06
rope_base = 1000000.0
MASKED = -1e30
LOG2E = 1.4426950408889634
OUT_HEADS = 2
FIRST_HEADS = 2
VMEM = 24 * 1024 * 1024

NT = (((1,), (1,)), ((), ()))
NN = (((1,), (0,)), ((), ()))
TN = (((0,), (0,)), ((), ()))


def dot(a, b, dims):
    return lax.dot_general(a, b, dims, preferred_element_type=jnp.float32)


def roll_half(x):
    return pltpu.roll(x, HALF, axis=1)


def unrotate(grad, cosine, sine):
    return grad * cosine - roll_half(grad) * sine


def swap_halves(x):
    return jnp.concatenate([x[HALF:], x[:HALF]], axis=0)


def beside_heads(x):
    return jnp.concatenate([x[h * HEAD_DIM:(h + 1) * HEAD_DIM] for h in range(GROUP)], axis=1)


def over_heads(x):
    return jnp.concatenate([x[:, h * ROWS:(h + 1) * ROWS] for h in range(GROUP)], axis=0)


def fold8(x):
    return jnp.sum(x.reshape(x.shape[0] // 8, 8, x.shape[1]), axis=0)


def stack_heads(x):
    return jnp.concatenate([x[:, h * HEAD_DIM:(h + 1) * HEAD_DIM] for h in range(GROUP)], axis=0)


def table_kernel(len_ref, place_ref, freq_ref, q_in, do_in, table_ref, row_ref, q_ref, do_ref, sems):
    copies = [
        pltpu.make_async_copy(source.at[:, pl.ds(0, target.shape[1])], target, sems.at[n])
        for n, (source, target) in enumerate(((q_in, q_ref), (do_in, do_ref)))
    ]
    for copy in copies:
        copy.start()
    base = place_ref[0]
    freqs = freq_ref[...]
    token = lax.broadcasted_iota(jnp.int32, (ROWS, HEAD_DIM), 0) + base
    angles = token.astype(jnp.float32) * freqs
    table_ref[0] = jnp.cos(angles)
    table_ref[1] = signed(jnp.sin(angles))

    here = lax.broadcasted_iota(jnp.int32, (8, ROWS), 1)
    first = jnp.zeros((8, ROWS), jnp.int32) - base
    end = -base
    for k in range(len_ref.shape[0] - 1):
        end = end + len_ref[k]
        first = jnp.where(here >= end, end, first)
    row_ref[0] = first.astype(jnp.float32)
    for n in (1, 2):
        angle = jnp.broadcast_to(freqs * float(n * ROWS), (8, HEAD_DIM))
        row_ref[2 * n - 1] = jnp.cos(angle)
        row_ref[2 * n] = signed(jnp.sin(angle))
    for copy in copies:
        copy.wait()


def signed(sine):
    lane = lax.broadcasted_iota(jnp.int32, sine.shape, 1)
    return jnp.where(lane < HALF, -sine, sine)


SMEM_IN = pl.BlockSpec(memory_space=pltpu.SMEM)
VMEM_IN = pl.BlockSpec(memory_space=pltpu.VMEM)
HBM_IN = pl.BlockSpec(memory_space=pltpu.HBM)


def in_hbm(*arrays):
    return [pltpu.with_memory_space_constraint(a, pltpu.HBM) for a in arrays]


def block_tables(lengths, place, q, do):
    half = rope_base ** (-np.arange(HALF) * 2.0 / HEAD_DIM)
    freqs = jnp.asarray(np.concatenate([half, half])[None], jnp.float32)
    return pl.pallas_call(
        table_kernel,
        in_specs=[SMEM_IN, SMEM_IN, VMEM_IN, HBM_IN, HBM_IN],
        out_specs=[VMEM_IN] * 4,
        out_shape=[
            pltpu.VMEM((2, ROWS, HEAD_DIM), jnp.float32),
            pltpu.VMEM((5, 8, HEAD_DIM), jnp.float32),
            pltpu.VMEM((ROWS, FIRST_HEADS * GROUP * HEAD_DIM), q.dtype),
            pltpu.VMEM((ROWS, FIRST_HEADS * GROUP * HEAD_DIM), q.dtype),
        ],
        scratch_shapes=[pltpu.SemaphoreType.DMA((2,))],
        compiler_params=pltpu.CompilerParams(vmem_limit_bytes=VMEM),
        name="tables",
    )(lengths, place, freqs, *in_hbm(q, do))


def pack_kernel(k_ref, v_ref, qg_in, kg_in, shard_ref, own_ref, gain_out, gain_ref, qg_ref, kg_ref, sems):
    copies = [
        pltpu.make_async_copy(
            ref.at[:, pl.ds(h * HEAD_DIM, HEAD_DIM)],
            own_ref.at[:, pl.ds((2 * h + n) * HEAD_DIM, HEAD_DIM)],
            sems.at[2 * h + n],
        )
        for h in range(KV_HEADS) for n, ref in enumerate((k_ref, v_ref))
    ]
    gains = [
        pltpu.make_async_copy(source, target, sems.at[2 * KV_HEADS + n])
        for n, (source, target) in enumerate(((qg_in, qg_ref), (kg_in, kg_ref)))
    ]
    for copy in gains + copies:
        copy.start()
    for copy in gains:
        copy.wait()
    width = qg_ref.shape[0]
    lane = lax.broadcasted_iota(jnp.int32, (2, HEAD_DIM), 1) - shard_ref[0] * width
    row = lax.broadcasted_iota(jnp.int32, (2, HEAD_DIM), 0)
    both = jnp.zeros((2, HEAD_DIM), jnp.float32)
    for i in range(width):
        both = jnp.where(lane == i, jnp.where(row == 0, qg_ref[i], kg_ref[i]), both)
    gain_ref[...] = jnp.broadcast_to(both[None], gain_ref.shape)
    copies.append(pltpu.make_async_copy(gain_ref, gain_out, sems.at[2 * KV_HEADS + 2]))
    copies[-1].start()
    for copy in copies:
        copy.wait()


def pack(k, v, q_gain, k_gain, shard, shards):
    return pl.pallas_call(
        pack_kernel,
        in_specs=[HBM_IN] * 4 + [SMEM_IN],
        out_specs=[VMEM_IN, HBM_IN],
        out_shape=[
            pltpu.VMEM((ROWS, 2 * KV_HEADS * HEAD_DIM), jnp.bfloat16),
            pltpu.HBM((shards, 2, HEAD_DIM), jnp.float32),
        ],
        scratch_shapes=[
            pltpu.VMEM((shards, 2, HEAD_DIM), jnp.float32),
            pltpu.SMEM(q_gain.shape, jnp.float32),
            pltpu.SMEM(k_gain.shape, jnp.float32),
            pltpu.SemaphoreType.DMA((2 * KV_HEADS + 3,)),
        ],
        compiler_params=pltpu.CompilerParams(vmem_limit_bytes=VMEM),
        name="pack",
    )(*in_hbm(k, v, q_gain, k_gain), shard)


def forward_keys(raw, gain, cosine, sine):
    x = raw.astype(jnp.float32)
    unit = x * lax.rsqrt(jnp.mean(x * x, axis=-1, keepdims=True) + norm_epsilon)
    straight, across = unit * cosine, roll_half(unit) * sine
    return straight, across, (straight * gain + across * roll_half(gain)).astype(jnp.bfloat16)


def over(a, b):
    return jnp.concatenate([a, b], axis=0)


def beside(a, b):
    return jnp.concatenate([a, b], axis=1)


def wide(a):
    return jnp.concatenate([a] * GROUP, axis=1)


def tall(a):
    return jnp.concatenate([a] * GROUP, axis=0)


def attend_kernel(
    q_first, do_first, q_in, do_in, own_ref, one_ref, two_ref, table_ref, row_ref, gain_ref,
    dq_out, ret1_out, ret2_out, keep_ref, gains_out, gains_ref, q_rest, do_rest, dq_ref, ret1_ref, ret2_ref, q_total, k_total, in_sems, sems,
):
    group, pair = GROUP * HEAD_DIM, 2 * HEAD_DIM

    ahead = q_first.shape[1]
    fetch = [
        pltpu.make_async_copy(source.at[:, pl.ds(ahead, target.shape[1])], target, in_sems.at[n])
        for n, (source, target) in enumerate(((q_in, q_rest), (do_in, do_rest)))
    ]
    for copy in fetch:
        copy.start()

    gain = jnp.sum(gain_ref[...], axis=0)
    kg = gain[1:2]
    qgt = jnp.broadcast_to(gain[0:1], (HEAD_DIM, HEAD_DIM)).T
    cos0, sin0 = table_ref[0], table_ref[1]
    cost, sint = cos0.T, sin0.T
    turn, cross, uncross = wide(qgt * cost), wide(swap_halves(qgt) * sint), wide(qgt * sint)

    row = lax.broadcasted_iota(jnp.int32, (ROWS, ROWS), 0).astype(jnp.float32)
    lane = lax.broadcasted_iota(jnp.int32, (ROWS, ROWS), 1).astype(jnp.float32)
    first = jnp.concatenate([row_ref[0]] * (ROWS // 8), axis=0)
    late_f = jnp.where(first < -ROWS, 1.0, 0.0)
    latet = wide(late_f.astype(jnp.bfloat16))
    on_timet = wide((1.0 - late_f).astype(jnp.bfloat16))
    late_f = late_f.T
    late = tall(late_f.astype(jnp.bfloat16))
    on_time = tall((1.0 - late_f).astype(jnp.bfloat16))
    take = row >= jnp.broadcast_to(first[:, 0:1], row.shape) + 2 * ROWS
    own = (row <= lane) & (row >= first)
    bias = over(
        wide(jnp.where(row >= first + ROWS, 0.0, MASKED)),
        wide(jnp.where(own | (row >= first + 2 * ROWS), 0.0, MASKED)),
    )

    def back(n):
        cosine, sine = row_ref[2 * n - 1][0:1], row_ref[2 * n][0:1]
        return cos0 * cosine + sin0 * sine, sin0 * cosine - cos0 * sine

    cos1, sin1 = back(1)
    cos2, sin2 = back(2)
    cos2, sin2 = jnp.where(take, cos2, cos0), jnp.where(take, sin2, sin0)
    q_total[...] = jnp.zeros_like(q_total)
    k_total[...] = jnp.zeros_like(k_total)

    def out(step):
        copies = []
        for n, (source, target) in enumerate(((dq_ref, dq_out), (ret1_ref, ret1_out), (ret2_ref, ret2_out))):
            width = OUT_HEADS * (group if n == 0 else pair)
            at = pl.ds(step * width, width)
            copies.append(pltpu.make_async_copy(source.at[:, at], target.at[:, at], sems.at[n, step]))
        return copies

    def one_head(head):
        heads = slice(head * group, (head + 1) * group)
        at_k = slice(head * pair, head * pair + HEAD_DIM)
        at_v = slice(head * pair + HEAD_DIM, (head + 1) * pair)
        among = heads
        q_ref, do_ref = q_first, do_first
        if head >= FIRST_HEADS:
            among = slice(head * group - ahead, (head + 1) * group - ahead)
            q_ref, do_ref = q_rest, do_rest
        xt = beside_heads(q_ref[:, among].T).astype(jnp.float32)
        inv_q = lax.rsqrt(jnp.mean(xt * xt, axis=0, keepdims=True) + norm_epsilon)
        qt = ((xt * turn + swap_halves(xt) * cross) * inv_q).astype(jnp.bfloat16)
        q = jnp.concatenate([qt[:, h * ROWS:(h + 1) * ROWS].T for h in range(GROUP)], axis=0)
        do = stack_heads(do_ref[:, among])
        dot_ = beside_heads(do_ref[:, among].T)
        qt_wide = over(qt * on_timet, qt * latet)
        dot_wide = over(dot_ * on_timet, dot_ * latet)
        q_wide = beside(q * on_time, q * late)
        do_wide = beside(do * on_time, do * late)

        v0, v1 = own_ref[:, at_v], one_ref[:, at_v]
        v2 = jnp.where(take, two_ref[:, at_v], v0)
        straight0, across0, k0 = forward_keys(own_ref[:, at_k], kg, cos0, sin0)
        straight1, across1, k1 = forward_keys(one_ref[:, at_k], kg, cos1, sin1)
        straight2, across2, k2 = forward_keys(jnp.where(take, two_ref[:, at_k], own_ref[:, at_k]), kg, cos2, sin2)
        k_all = over(beside(k1, k1), beside(k0, k2))
        v_all = over(beside(v1, v1), beside(v0, v2))
        k1t = k1.T
        kt_all = over(beside(k1t, k0.T), beside(k1t, k2.T))

        s = dot(k_all, qt_wide, NN) * (HEAD_DIM ** (-0.5) * LOG2E) + bias
        w = jnp.exp2(s - jnp.max(s, axis=0, keepdims=True))
        p = w * (1.0 / jnp.sum(w, axis=0, keepdims=True))
        dp = dot(v_all, dot_wide, NN)
        delta = jnp.sum(p * dp, axis=0, keepdims=True)
        ds = (p * (dp - delta) * (HEAD_DIM ** (-0.5))).astype(jnp.bfloat16)

        dv = dot(p.astype(jnp.bfloat16), do_wide, NN)
        dk = dot(ds, q_wide, NN)
        dk1, dv1 = dk[:ROWS, :HEAD_DIM] + dk[:ROWS, HEAD_DIM:], dv[:ROWS, :HEAD_DIM] + dv[:ROWS, HEAD_DIM:]
        dk0, dk2 = dk[ROWS:, :HEAD_DIM], dk[ROWS:, HEAD_DIM:]
        dv0, dv2 = dv[ROWS:, :HEAD_DIM], dv[ROWS:, HEAD_DIM:]

        dqt = dot(kt_all, ds, NN)
        dqt = jnp.where(latet > 0.0, dqt[HEAD_DIM:], dqt[:HEAD_DIM])
        dqt = dqt.astype(jnp.bfloat16).astype(jnp.float32)
        et = dqt * turn - swap_halves(dqt) * uncross
        ext = et * xt
        mean = jnp.mean(ext, axis=0, keepdims=True)
        dxt = (et * inv_q - xt * (inv_q * inv_q * inv_q * mean)).astype(jnp.bfloat16)
        dq_ref[:, heads] = over_heads(dxt).T
        ext = ext * inv_q
        q_total[...] += sum(ext[:, h * ROWS:(h + 1) * ROWS] for h in range(GROUP))
        k_total[0] += fold8(dk0 * straight0 + dk1 * straight1 + dk2 * straight2)
        k_total[1] += fold8(dk0 * across0 + dk1 * across1 + dk2 * across2)

        ret1_ref[:, at_k] = dk1.astype(jnp.bfloat16)
        ret1_ref[:, at_v] = dv1.astype(jnp.bfloat16)
        ret2_ref[:, at_k] = jnp.where(take, dk2, 0.0).astype(jnp.bfloat16)
        ret2_ref[:, at_v] = jnp.where(take, dv2, 0.0).astype(jnp.bfloat16)
        keep_ref[:, at_k] = dk0 + jnp.where(take, 0.0, dk2)
        keep_ref[:, at_v] = dv0 + jnp.where(take, 0.0, dv2)

    for head in range(KV_HEADS):
        if head == FIRST_HEADS:
            for copy in fetch:
                copy.wait()
        one_head(head)
        if head % OUT_HEADS == OUT_HEADS - 1:
            for copy in out(head // OUT_HEADS):
                copy.start()

    q_gain_grad = jnp.sum(q_total[...].T, axis=0, keepdims=True) / gain[0:1]
    k_gain_grad = jnp.sum(k_total[0] + roll_half(k_total[1]), axis=0, keepdims=True)
    gains_ref[...] = jnp.broadcast_to(over(q_gain_grad, k_gain_grad)[None], gains_ref.shape)
    gains = pltpu.make_async_copy(gains_ref, gains_out, in_sems.at[2])
    gains.start()

    for step in range(KV_HEADS // OUT_HEADS):
        for copy in out(step):
            copy.wait()
    gains.wait()


def attend(q_first, do_first, q, do, own, one, two, tables, peers):
    pair = (ROWS, 2 * KV_HEADS * HEAD_DIM)
    return pl.pallas_call(
        attend_kernel,
        in_specs=[VMEM_IN] * 2 + [HBM_IN] * 2 + [VMEM_IN] * 6,
        out_specs=[HBM_IN] * 3 + [VMEM_IN, HBM_IN],
        out_shape=[
            pltpu.HBM(q.shape, jnp.bfloat16),
            pltpu.HBM(pair, jnp.bfloat16),
            pltpu.HBM(pair, jnp.bfloat16),
            pltpu.VMEM(pair, jnp.float32),
            pltpu.HBM((peers, 2, HEAD_DIM), jnp.float32),
        ],
        scratch_shapes=[
            pltpu.VMEM((peers, 2, HEAD_DIM), jnp.float32),
            pltpu.VMEM((ROWS, q.shape[1] - q_first.shape[1]), jnp.bfloat16),
            pltpu.VMEM((ROWS, q.shape[1] - q_first.shape[1]), jnp.bfloat16),
            pltpu.VMEM(q.shape, jnp.bfloat16),
            pltpu.VMEM(pair, jnp.bfloat16),
            pltpu.VMEM(pair, jnp.bfloat16),
            pltpu.VMEM((HEAD_DIM, HEAD_DIM), jnp.float32),
            pltpu.VMEM((2, 8, HEAD_DIM), jnp.float32),
            pltpu.SemaphoreType.DMA((3,)),
            pltpu.SemaphoreType.DMA((3, KV_HEADS // OUT_HEADS)),
        ],
        compiler_params=pltpu.CompilerParams(vmem_limit_bytes=VMEM),
        name="attend",
    )(q_first, do_first, *in_hbm(q, do), own, one, two, *tables)


def hint(work):
    return pl.CostEstimate(flops=work * 20_000_000_000, bytes_accessed=work * 40_000_000, transcendentals=0)


def add_up_kernel(parts_ref, out_ref):
    total = jnp.sum(parts_ref[...], axis=0, keepdims=True)
    out_ref[...] = jnp.broadcast_to(total, out_ref.shape)


def add_up(parts, peers, ahead):
    return pl.pallas_call(
        add_up_kernel,
        in_specs=[VMEM_IN],
        out_specs=VMEM_IN,
        out_shape=jax.ShapeDtypeStruct((peers,) + parts.shape[1:], parts.dtype),
        compiler_params=pltpu.CompilerParams(vmem_limit_bytes=VMEM),
        cost_estimate=hint(ahead),
        name="add_up",
    )(parts)


def merge_kernel(odd_ref, near_ref, ret_in, keep_in, far_ref, keep_ref, ret_ref, sems):
    pieces = sems.shape[0]
    width = near_ref.shape[1] // pieces
    odd = odd_ref[0].astype(jnp.float32)

    def fetch(n):
        at = pl.ds(n * width, width)
        return pltpu.make_async_copy(ret_in.at[:, at], ret_ref.at[:, at], sems.at[n])

    for n in range(pieces):
        fetch(n).start()
    for n in range(pieces):
        at = pl.ds(n * width, width)
        near = near_ref[:, at].astype(jnp.float32)
        fetch(n).wait()
        far_ref[:, at] = (ret_ref[:, at] + near * odd).astype(jnp.bfloat16)
        keep_ref[:, at] = keep_in[:, at] + near * (1.0 - odd)


def merge(odd, near, ret, keep):
    pieces = 4
    return pl.pallas_call(
        merge_kernel,
        in_specs=[SMEM_IN, VMEM_IN, HBM_IN, VMEM_IN],
        out_specs=[VMEM_IN] * 2,
        out_shape=[pltpu.VMEM(ret.shape, ret.dtype), pltpu.VMEM(keep.shape, keep.dtype)],
        input_output_aliases={3: 1},
        scratch_shapes=[
            pltpu.VMEM(ret.shape, ret.dtype),
            pltpu.SemaphoreType.DMA((pieces,)),
        ],
        compiler_params=pltpu.CompilerParams(vmem_limit_bytes=VMEM),
        name="merge",
    )(odd.astype(jnp.int32)[None], near, *in_hbm(ret), keep)


def finish_kernel(own_ref, keep_ref, far_ref, table_ref, gain_ref, dk_ref, dv_ref, stage, sems):
    gain = jnp.sum(gain_ref[...], axis=0)[1:2]
    copies = []
    for h in range(KV_HEADS):
        at_k, at_v = pl.ds(2 * h * HEAD_DIM, HEAD_DIM), pl.ds((2 * h + 1) * HEAD_DIM, HEAD_DIM)
        dk, dv = (keep_ref[:, at] + far_ref[:, at] for at in (at_k, at_v))
        x = own_ref[:, at_k].astype(jnp.float32)
        inverse = lax.rsqrt(jnp.mean(x * x, axis=-1, keepdims=True) + norm_epsilon)
        dk = dk.astype(jnp.bfloat16).astype(jnp.float32)
        e = unrotate(dk, table_ref[0], table_ref[1]) * gain
        mean = jnp.mean(e * x, axis=-1, keepdims=True)
        stage[0, h] = (inverse * (e - x * (inverse * inverse * mean))).astype(jnp.bfloat16)
        stage[1, h] = dv.astype(jnp.bfloat16)
        for n, ref in enumerate((dk_ref, dv_ref)):
            at = pl.ds(h * HEAD_DIM, HEAD_DIM)
            copies.append(pltpu.make_async_copy(stage.at[n, h], ref.at[:, at], sems.at[n, h]))
            copies[-1].start()
    for copy in copies:
        copy.wait()


def finish(own, keep, far, table, gain):
    out = jax.ShapeDtypeStruct((ROWS, KV_HEADS * HEAD_DIM), jnp.bfloat16)
    return pl.pallas_call(
        finish_kernel,
        in_specs=[VMEM_IN] * 5,
        out_specs=[HBM_IN] * 2,
        out_shape=[out, out],
        scratch_shapes=[
            pltpu.VMEM((2, KV_HEADS, ROWS, HEAD_DIM), jnp.bfloat16),
            pltpu.SemaphoreType.DMA((2, KV_HEADS)),
        ],
        compiler_params=pltpu.CompilerParams(vmem_limit_bytes=VMEM),
        name="finish",
    )(own, keep, far, table, gain)


AXES = ("seq", "fsdp")


def device_at(y, z, x, core):
    return ((y % 4 * 4 + x) * 2 + core) * 16 + y // 4 * 8 + z


def gain_groups():
    return [
        [device_at(a, z, x, c) for z in range(8)] + [device_at(4 + (a + 2) % 4, z, x, c) for z in range(8)]
        for a in range(4) for x in range(4) for c in range(2)
    ]


def plane_groups():
    return [[device_at(y, z, x, c) for y in range(8) for x in range(4) for c in range(2)] for z in range(8)]


def column_groups():
    return [[device_at(y, z, x, c) for z in range(8)] for y in range(8) for x in range(4) for c in range(2)]


def swap(rows, groups):
    return lax.all_to_all(rows, AXES, 0, 0, axis_index_groups=groups, tiled=True)


def local(query_raw, key_raw, value_proj, out_grad, query_gain, key_gain, turn_lengths):
    me, shard = lax.axis_index("seq"), lax.axis_index("fsdp")
    seq, shards = lax.axis_size("seq"), lax.axis_size("fsdp")
    base = me * ROWS
    odd = me % 2 == 1

    own, gain = pack(key_raw[0], value_proj[0], query_gain, key_gain, shard[None], shards)
    table, rows, q_first, do_first = block_tables(turn_lengths[0], base[None], query_raw[0], out_grad[0])
    two = lax.ppermute(own, "seq", [(i, i + 2) for i in range(seq - 2)])
    gain = add_up(swap(gain, gain_groups()), 1, 1)
    one = jnp.where(odd, two, own)
    one, table = lax.optimization_barrier((one, table))
    one = lax.ppermute(one, "seq", [(i, i ^ 1) for i in range(seq)])
    q_grad, ret1, ret2, keep, parts = attend(q_first, do_first, query_raw[0], out_grad[0], own, one, two, (table, rows, gain), 64)

    near = lax.ppermute(ret1, "seq", [(i, i ^ 1) for i in range(seq)])
    far, keep = merge(odd, near, ret2, keep)
    far = lax.ppermute(far, "seq", [(i + 2, i) for i in range(seq - 2)])
    part = add_up(swap(parts, plane_groups()), 8, 1)
    total = swap(part, column_groups())
    k_grad, v_grad = finish(own, keep, far, table, gain)
    total, k_grad, v_grad = lax.optimization_barrier((total, k_grad, v_grad))
    total = jnp.sum(total, axis=0)
    shard_rows = total.reshape(2, shards, HEAD_DIM // shards)
    gain_grad = lax.dynamic_slice_in_dim(shard_rows, shard, 1, axis=1)

    return q_grad[None], k_grad[None], v_grad[None], gain_grad[0, 0], gain_grad[1, 0]


def solution(mesh):
    return jax.shard_map(
        local,
        mesh=mesh,
        in_specs=(
            P("fsdp", "seq", None),
            P("fsdp", "seq", None),
            P("fsdp", "seq", None),
            P("fsdp", "seq", None),
            P("fsdp"),
            P("fsdp"),
            P("fsdp", None),
        ),
        out_specs=(
            P("fsdp", "seq", None),
            P("fsdp", "seq", None),
            P("fsdp", "seq", None),
            P("fsdp"),
            P("fsdp"),
        ),
        check_vma=False,
    )
```
